1024 devices in a mesh: rows: 128 (over z, x, core), tm: 8 (over y).
Axes of the slice: x: 8, y: 8, z: 8, core: 2. Of those that a mesh axis runs over, the one named last changes fastest.
Arguments:
- fields: float32 [5, 64, 1024, 4, 128], P(None, 'tm', 'rows'), may hold values from -23 to 23
- channel_mix: float32 [32, 35], replicated, may hold values from -1.5 to 2.5
Outputs:
- running_factor: float32 [8, 256, 256], P('tm')
- coefficients: bfloat16 [64, 32, 1024, 4, 128], P('tm', None, 'rows')
The draws below stay inside these ranges and needn't reach their ends.
All inputs are finite; a program needn't handle non-finite values.
Results may differ from the reference program's by a relative error of at most 0.0039.
The reference program's roundings to bfloat16 on the way count: a program that leaves them out, or rounds other values in their place, can miss the bound.
Values sent between devices are 32-bit elements; how exact they have to be, the bound alone decides.
A program may use at most 128 MiB of HBM per device.

```python
import jax
import jax.numpy as jnp
from jax import lax

FIELDS = 5
STENCILS = 7
CH = 32
SNAP_GRP = 8
NY = 4
NZ = 128
FEAT = 256
NX = 1024
SNAPS = 64
N_TM = 8


def draw_fields(key, part):
    first_key, second_key, third_key, fourth_key = jax.random.split(key, 4)
    common = jax.random.truncated_normal(first_key, -4.0, 4.0, (FIELDS, 1, NX, NY, NZ), jnp.float32)
    scales = jnp.exp(jax.random.uniform(third_key, (FIELDS, 1, NX, NY, NZ), jnp.float32, -0.6, 0.6))
    position = jnp.arange(SNAPS).astype(jnp.float32) / jnp.float32(max(SNAPS - 1, 1))
    jitter = jnp.exp(jax.random.uniform(fourth_key, (FIELDS, SNAPS, 1, 1, 1), jnp.float32, -0.4, 0.4))
    amplitude = (0.5 + position).reshape(1, SNAPS, 1, 1, 1) * jitter
    fresh = jax.random.truncated_normal(second_key, -4.0, 4.0, (FIELDS, SNAPS, NX, NY, NZ), jnp.float32)
    values = (0.6 * common + 0.8 * fresh) * scales * amplitude
    return values


def draw_channel_mix(key, part):
    identity = jnp.eye(CH, FIELDS * STENCILS, dtype=jnp.float32)
    spread = 0.35 * jax.random.truncated_normal(key, -4.0, 4.0, (CH, FIELDS * STENCILS), jnp.float32)
    return identity + spread


def setup_inputs(seed: int = 0) -> dict:
    key_list = jax.random.split(jax.random.key(seed), 3)
    return {
        "fields": draw_fields(jax.random.fold_in(key_list[2], 71), 0),
        "channel_mix": draw_channel_mix(jax.random.fold_in(key_list[2], 71), 0),
    }


def derivatives(padded):
    center = padded[:, :, 1:-1, 1:-1, 1:-1]
    x_plus = padded[:, :, 2:, 1:-1, 1:-1]
    x_minus = padded[:, :, :-2, 1:-1, 1:-1]
    y_plus = padded[:, :, 1:-1, 2:, 1:-1]
    y_minus = padded[:, :, 1:-1, :-2, 1:-1]
    z_plus = padded[:, :, 1:-1, 1:-1, 2:]
    z_minus = padded[:, :, 1:-1, 1:-1, :-2]
    stacked = jnp.stack([center, 0.5 * (x_plus - x_minus), 0.5 * (y_plus - y_minus), 0.5 * (z_plus - z_minus), 0.25 * (x_plus - 2.0 * center + x_minus), 0.25 * (y_plus - 2.0 * center + y_minus), 0.25 * (z_plus - 2.0 * center + z_minus)], axis=1)
    shape = stacked.shape
    return stacked.reshape((shape[0] * shape[1],) + shape[2:])

def reference(fields, channel_mix):
    cells = NX * NY * NZ
    summed = jnp.zeros((FEAT, FEAT), jnp.float32)
    factors = []
    blocks = []
    for interval in range(N_TM):
        section = fields[:, interval * SNAP_GRP:(interval + 1) * SNAP_GRP]
        padded = jnp.pad(section, ((0, 0), (0, 0), (1, 1), (1, 1), (1, 1)))
        stencil = derivatives(padded)
        channels = jnp.einsum('ck,ksxyz->scxyz', channel_mix, stencil, precision=lax.Precision.HIGHEST).astype(jnp.bfloat16)
        features = channels.reshape(FEAT, cells)
        gram = jnp.dot(features.astype(jnp.float32), features.T.astype(jnp.float32), preferred_element_type=jnp.float32)
        summed = summed + gram
        lower = jnp.linalg.cholesky(summed / jnp.float32((interval + 1) * cells))
        factors.append(lower)
        solved = lax.linalg.triangular_solve(lower, features.astype(jnp.float32), left_side=True, lower=True)
        blocks.append(solved.reshape(channels.shape).astype(jnp.bfloat16))
    return (jnp.stack(factors, axis=0), jnp.concatenate(blocks, axis=0))
```

```python
import functools
import math

import jax
import jax.numpy as jnp
from jax import lax
from jax.experimental import pallas as pl
from jax.experimental.pallas import tpu as pltpu
from jax.sharding import PartitionSpec as P

MESH = pl.DeviceIdType.MESH


def padded_2(cells, sides, width):
    for axis, dim in sides:
        count = lax.axis_size(axis)
        ends = count - 1
        head = lax.slice_in_dim(cells, 0, width, axis=dim)
        tail = lax.slice_in_dim(cells, cells.shape[dim] - width, cells.shape[dim], axis=dim)
        cells = jnp.concatenate(
            [
                lax.ppermute(tail, axis, [(i, (i + 1) % count) for i in range(ends)]),
                cells,
                lax.ppermute(head, axis, [((i + 1) % count, i) for i in range(ends)]),
            ],
            axis=dim,
        )
    return cells


def derivatives(padded):
    center = padded[:, :, 1:-1, 1:-1, 1:-1]
    x_plus = padded[:, :, 2:, 1:-1, 1:-1]
    x_minus = padded[:, :, :-2, 1:-1, 1:-1]
    y_plus = padded[:, :, 1:-1, 2:, 1:-1]
    y_minus = padded[:, :, 1:-1, :-2, 1:-1]
    z_plus = padded[:, :, 1:-1, 1:-1, 2:]
    z_minus = padded[:, :, 1:-1, 1:-1, :-2]
    stacked = jnp.stack(
        [
            center,
            0.5 * (x_plus - x_minus),
            0.5 * (y_plus - y_minus),
            0.5 * (z_plus - z_minus),
            0.25 * (x_plus - 2.0 * center + x_minus),
            0.25 * (y_plus - 2.0 * center + y_minus),
            0.25 * (z_plus - 2.0 * center + z_minus),
        ],
        axis=1,
    )
    shape = stacked.shape
    return stacked.reshape((shape[0] * shape[1],) + shape[2:])


def running_kernel(
    side, steps, gram_ref, out_ref,
    stack, pair_in, mine, got_a, got_b, got_y, whole,
    pair_send, pair_recv, a_send, a_recv, b_send, b_recv,
    y_send, y_recv, g_send, g_recv, f_send, f_recv,
):
    here = lax.axis_index("rows")
    t = lax.axis_index("tm")
    core = here % 2
    chip = here // 2
    z, x = chip // side, chip % side
    a = (1 - core) * x + core * z
    b = (1 - core) * z + core * x
    a_step = (1 - core) + core * side
    b_step = (1 - core) * side + core
    half = stack.shape[1]
    piece = half // side

    def at_a(k):
        return {"rows": 2 * (k * a_step + b * b_step) + core}

    def at_b(k):
        return {"rows": 2 * (a * a_step + k * b_step) + core}

    def at_t(k):
        return {"tm": k}

    partner = {"rows": 2 * chip + 1 - core}

    def copy(src, dst, send, recv, to):
        return pltpu.make_async_remote_copy(
            src_ref=src, dst_ref=dst, send_sem=send, recv_sem=recv,
            device_id=to, device_id_type=MESH,
        )

    barrier = pltpu.get_barrier_semaphore()
    pl.semaphore_signal(barrier, inc=1, device_id=partner, device_id_type=MESH)
    for d in range(1, side):
        pl.semaphore_signal(barrier, inc=1, device_id=at_a((a + d) % side), device_id_type=MESH)
        pl.semaphore_signal(barrier, inc=1, device_id=at_b((b + d) % side), device_id_type=MESH)
    for d in range(1, steps):
        pl.semaphore_signal(barrier, inc=1, device_id=at_t((t + d) % steps), device_id_type=MESH)

    edge = gram_ref.shape[0] // 2
    flat = [gram_ref[:edge, :edge], gram_ref[edge:, :edge], gram_ref[edge:, edge:]]
    cut = edge // 2
    stack[0, :edge] = flat[0]
    stack[0, edge:] = flat[1][:cut]
    stack[1, :cut] = flat[1][cut:]
    stack[1, cut:] = flat[2]

    pl.semaphore_wait(barrier, 2 * (side - 1) + steps)

    sends = []
    pair = copy(stack.at[1 - core], pair_in, pair_send, pair_recv, partner)
    pair.start()
    sends.append(pair)
    pair.wait_recv()
    mine[...] = (stack[core] + pair_in[...]).reshape(mine.shape)

    for d in range(1, side):
        k = (a + d) % side
        c = copy(mine.at[k], got_a.at[a], a_send.at[d], a_recv.at[a], at_a(k))
        c.start()
        sends.append(c)
    total = mine[a]
    for d in range(1, side):
        k = (a + d) % side
        copy(mine.at[a], got_a.at[k], a_send.at[d], a_recv.at[k], at_a(k)).wait_recv()
        total = total + got_a[k]
    got_b[b] = total

    for d in range(1, side):
        k = (b + d) % side
        c = copy(got_b.at[b], got_b.at[b], b_send.at[d], b_recv.at[b], at_b(k))
        c.start()
        sends.append(c)
    for d in range(1, side):
        k = (b + d) % side
        copy(got_b.at[b], got_b.at[k], b_send.at[d], b_recv.at[k], at_b(k)).wait_recv()
    total = got_b[0]
    for k in range(1, side):
        total = total + got_b[k]
    got_y[t] = total

    for d in range(1, steps):
        k = t + d

        @pl.when(k < steps)
        def _():
            copy(got_y.at[t], got_y.at[t], y_send.at[d], y_recv.at[t], at_t(k)).start()

    whole[core, a] = jnp.zeros_like(total)
    for k in range(steps):

        @pl.when(k < t)
        def _():
            copy(got_y.at[k], got_y.at[k], y_send.at[0], y_recv.at[k], at_t(k)).wait_recv()

        @pl.when(k <= t)
        def _():
            whole[core, a] += got_y[k]

    def forward(k):
        return copy(whole.at[core, k], whole.at[core, k], f_send.at[k], f_recv.at[k], partner)

    for d in range(1, side):
        k = (a + d) % side
        c = copy(whole.at[core, a], whole.at[core, a], g_send.at[d], g_recv.at[a], at_a(k))
        c.start()
        sends.append(c)
    c = forward(a)
    c.start()
    sends.append(c)
    for d in range(1, side):
        k = (a + d) % side
        copy(whole.at[core, a], whole.at[core, k], g_send.at[d], g_recv.at[k], at_a(k)).wait_recv()
        c = forward(k)
        c.start()
        sends.append(c)
    for k in range(side):
        copy(
            whole.at[core, k], whole.at[1 - core, k], f_send.at[k], f_recv.at[k], partner
        ).wait_recv()

    first = whole[0].reshape(half, edge)
    second = whole[1].reshape(half, edge)
    out_ref[:edge, :edge] = first[:edge]
    out_ref[edge:edge + cut, :edge] = first[edge:]
    out_ref[edge + cut:, :edge] = second[:cut]
    out_ref[edge:, edge:] = second[cut:]
    out_ref[:edge, edge:] = jnp.concatenate([first[edge:], second[:cut]], axis=0).T

    for c in sends:
        c.wait_send()
    for d in range(1, steps):
        k = t + d

        @pl.when(k < steps)
        def _():
            copy(got_y.at[t], got_y.at[t], y_send.at[d], y_recv.at[t], at_t(k)).wait_send()


def running_sum(gram):
    side = math.isqrt(lax.axis_size("rows") // 2)
    steps = lax.axis_size("tm")
    width = gram.shape[0]
    edge = width // 2
    half = 3 * edge // 2
    piece = half // side
    dma = pltpu.SemaphoreType.DMA
    f32 = jnp.float32
    return pl.pallas_call(
        functools.partial(running_kernel, side, steps),
        out_shape=jax.ShapeDtypeStruct((width, width), f32),
        in_specs=[pl.BlockSpec(memory_space=pltpu.VMEM)],
        out_specs=pl.BlockSpec(memory_space=pltpu.VMEM),
        scratch_shapes=[
            pltpu.VMEM((2, half, edge), f32),
            pltpu.VMEM((half, edge), f32),
            pltpu.VMEM((side, piece, edge), f32),
            pltpu.VMEM((side, piece, edge), f32),
            pltpu.VMEM((side, piece, edge), f32),
            pltpu.VMEM((steps, piece, edge), f32),
            pltpu.VMEM((2, side, piece, edge), f32),
            dma, dma,
            dma((side,)), dma((side,)),
            dma((side,)), dma((side,)),
            dma((steps,)), dma((steps,)),
            dma((side,)), dma((side,)),
            dma((side,)), dma((side,)),
        ],
        compiler_params=pltpu.CompilerParams(collective_id=0, has_side_effects=True),
    )(gram)


def body(fields, channel_mix):
    grown = padded_2(fields, (("rows", 2),), 1)
    padded = jnp.pad(grown, ((0, 0), (0, 0), (0, 0), (1, 1), (1, 1)))
    stencil = derivatives(padded)
    channels = jnp.einsum(
        "ck,ksxyz->scxyz", channel_mix, stencil, precision=lax.Precision.HIGHEST
    ).astype(jnp.bfloat16)
    width = channels.shape[0] * channels.shape[1]
    local_cells = channels.shape[2] * channels.shape[3] * channels.shape[4]
    features = channels.reshape(width, local_cells)
    gram = lax.dot_general(
        features, features, (((1,), (1,)), ((), ())), preferred_element_type=jnp.float32
    )
    running_gram = running_sum(gram)
    row_count = (lax.axis_index("tm") + 1).astype(jnp.float32) * jnp.float32(
        local_cells * lax.axis_size("rows")
    )
    factor = lax.linalg.cholesky(running_gram / row_count, symmetrize_input=False)
    solved = lax.linalg.triangular_solve(
        factor, features.astype(jnp.float32), left_side=True, lower=True
    )
    coefficients = solved.reshape(channels.shape).astype(jnp.bfloat16)
    return (factor[None], coefficients)


def solution(mesh):
    return jax.shard_map(
        body,
        mesh=mesh,
        in_specs=(P(None, "tm", "rows", None, None), P()),
        out_specs=(P("tm", None, None), P("tm", None, "rows", None, None)),
        check_vma=False,
    )
```

```python
import functools
import math

import jax
import jax.numpy as jnp
from jax import lax
from jax.experimental import pallas as pl
from jax.experimental.pallas import tpu as pltpu
from jax.sharding import PartitionSpec as P

MESH = pl.DeviceIdType.MESH
ROW, LANE, PANEL = 8, 128, 32


def parts(v):
    high = v.astype(jnp.bfloat16)
    rest = v - high.astype(jnp.float32)
    mid = rest.astype(jnp.bfloat16)
    low = (rest - mid.astype(jnp.float32)).astype(jnp.bfloat16)
    return high, mid, low


def eliminate(rows, col0, tiles):
    sub = lax.broadcasted_iota(jnp.int32, (ROW, LANE), 0)
    count = len(rows)

    def spread(v, q):
        return jnp.broadcast_to(v[q:q + 1, :], (ROW, LANE))

    for k in range(count):
        lane = (col0 + ROW * k) % LANE
        tc = tiles.index((col0 + ROW * k) // LANE)
        cols = [
            [jnp.broadcast_to(rows[i][tc][:, lane + q:lane + q + 1], (ROW, LANE)) for i in range(k, count)]
            for q in range(ROW)
        ]
        scale = jnp.zeros((ROW, LANE), jnp.float32)
        for q in range(ROW):
            pivot = spread(cols[q][0], q)
            inv = 1.0 / pivot
            scale = jnp.where(sub == q, lax.rsqrt(pivot), scale)
            mult = [c * inv for c in cols[q]]
            mult[0] = jnp.where(sub > q, mult[0], 0.0)
            for p in range(q + 1, ROW):
                line = spread(cols[p][0], q)
                cols[p] = [c - m * line for c, m in zip(cols[p], mult)]
            for t in range(len(tiles)):
                line = spread(rows[k][t], q)
                for i, m in enumerate(mult):
                    rows[k + i][t] = rows[k + i][t] - m * line
        for t in range(len(tiles)):
            rows[k][t] = rows[k][t] * scale
    return rows


def factor_kernel(gram_ref, feat_ref, fac_ref, out_ref, work, spread_out):
    n = gram_ref.shape[0]
    steps = n // PANEL
    work[:, :n] = gram_ref[...]
    eye_r = lax.broadcasted_iota(jnp.int32, (n, n), 0)
    eye_c = lax.broadcasted_iota(jnp.int32, (n, n), 1)
    work[:, n:] = jnp.where(eye_r == eye_c, 1.0, 0.0)
    left = n // LANE
    for p in range(steps):
        r0 = PANEL * p
        first = r0 // LANE
        tiles = list(range(first, left + first + 1))
        rows = [
            [work[r0 + ROW * i:r0 + ROW * (i + 1), LANE * t:LANE * (t + 1)] for t in tiles]
            for i in range(PANEL // ROW)
        ]
        rows = eliminate(rows, r0, tiles)
        whole = jnp.concatenate([jnp.concatenate(r, axis=1) for r in rows], axis=0)
        wide = LANE * (left - first)
        upper = whole[:, :wide]
        rr = r0 + lax.broadcasted_iota(jnp.int32, (PANEL, wide), 0)
        cc = LANE * first + lax.broadcasted_iota(jnp.int32, (PANEL, wide), 1)
        upper = jnp.where(cc >= rr, upper, 0.0)
        lower = upper.T
        fac_ref[LANE * first:, r0:r0 + PANEL] = lower
        if first:
            fac_ref[:LANE * first, r0:r0 + PANEL] = jnp.zeros((LANE * first, PANEL), jnp.float32)
        work[r0:r0 + PANEL, n:n + LANE * (first + 1)] = whole[:, wide:]
        r1 = r0 + PANEL
        if r1 < n:
            high, mid, low = parts(whole)
            right = jnp.concatenate([high, high, high, mid, mid, low], axis=0)
            lh, lm, ll = parts(lower)
            lhs = jnp.concatenate([lh, lm, ll, lh, lm, lh], axis=1)
            off = LANE * first
            for s0, s1 in ((r1, r1 + PANEL), (r1 + PANEL, n)):
                if s0 < s1:
                    change = jnp.dot(lhs[s0 - off:s1 - off], right, preferred_element_type=jnp.float32)
                    at = LANE * tiles[0]
                    work[s0:s1, at:at + LANE * len(tiles)] -= change
    inverse = work[:, n:]
    high = inverse.astype(jnp.bfloat16)
    mid = (inverse - high.astype(jnp.float32)).astype(jnp.bfloat16)
    cells = feat_ref.shape[1]
    blocks = cells // LANE
    chunk = 4
    for j in range(blocks // chunk):
        x = feat_ref[:, chunk * LANE * j:chunk * LANE * (j + 1)]
        y = jnp.dot(high, x, preferred_element_type=jnp.float32)
        y = y + jnp.dot(mid, x, preferred_element_type=jnp.float32)
        for b in range(chunk):
            spread_out[pl.ds(j * chunk + b, n, stride=blocks), :] = y[:, LANE * b:LANE * (b + 1)]
    out_ref[...] = spread_out[...].astype(jnp.bfloat16)


def factor_and_solve(gram, features):
    n, cells = features.shape
    lines = n * cells // LANE
    return pl.pallas_call(
        factor_kernel,
        out_shape=(
            jax.ShapeDtypeStruct((n, n), jnp.float32),
            jax.ShapeDtypeStruct((lines, LANE), jnp.bfloat16),
        ),
        in_specs=[pl.BlockSpec(memory_space=pltpu.VMEM)] * 2,
        out_specs=(pl.BlockSpec(memory_space=pltpu.VMEM),) * 2,
        scratch_shapes=[
            pltpu.VMEM((n, 2 * n), jnp.float32),
            pltpu.VMEM((lines, LANE), jnp.float32),
        ],
        compiler_params=pltpu.CompilerParams(vmem_limit_bytes=48 << 20),
    )(gram, features)


def spread_mix(mix, snaps, fields, rows):
    ch, count = mix.shape
    group = fields * snaps
    stencils = count // fields
    k = lax.broadcasted_iota(jnp.int32, (count, rows), 0)
    col = lax.broadcasted_iota(jnp.int32, (count, rows), 1)
    pick = (k // stencils == col % group // snaps) & (k % stencils == col // group)
    pick = jnp.where(pick, 1.0, 0.0).astype(jnp.bfloat16)
    r = lax.broadcasted_iota(jnp.int32, (snaps * ch, rows), 0)
    c = lax.broadcasted_iota(jnp.int32, (snaps * ch, rows), 1)
    same = r // ch == c % snaps
    out = []
    for part in parts(mix):
        wide = jnp.dot(part, pick, preferred_element_type=jnp.float32)
        wide = jnp.concatenate([wide] * snaps, axis=0)
        out.append(jnp.where(same, wide, 0.0).astype(jnp.bfloat16))
    return out


def front_kernel(dims, u_ref, lo_ref, hi_ref, mix_ref, feat_ref, gram_ref, weights):
    fields, snaps, nx, ny = dims
    fs = fields * snaps
    rows = 7 * fs + 8
    h, m, l = spread_mix(mix_ref[...], snaps, fields, rows)
    for i, w in enumerate((h, m, l, h, m, h)):
        weights[:, rows * i:rows * (i + 1)] = w
    lane = lax.broadcasted_iota(jnp.int32, (fs, LANE), 1)
    zero = jnp.zeros((fs, LANE), jnp.float32)
    pad = jnp.zeros((8, LANE), jnp.float32)

    def cell(x, y):
        if x < 0:
            return lo_ref[pl.ds(y, fs, stride=ny), :]
        if x >= nx:
            return hi_ref[pl.ds(y, fs, stride=ny), :]
        return u_ref[pl.ds(x * ny + y, fs, stride=nx * ny), :]

    for x in range(nx):
        here = [cell(x, y) for y in range(ny)]
        columns = []
        for y in range(ny):
            u = here[y]
            xp, xm = cell(x + 1, y), cell(x - 1, y)
            yp = here[y + 1] if y + 1 < ny else zero
            ym = here[y - 1] if y else zero
            zp = jnp.where(lane == LANE - 1, 0.0, pltpu.roll(u, LANE - 1, 1))
            zm = jnp.where(lane == 0, 0.0, pltpu.roll(u, 1, 1))
            twice = 2.0 * u
            stencil = jnp.concatenate(
                [
                    u,
                    0.5 * (xp - xm), 0.5 * (yp - ym), 0.5 * (zp - zm),
                    0.25 * (xp - twice + xm), 0.25 * (yp - twice + ym), 0.25 * (zp - twice + zm),
                    pad,
                ],
                axis=0,
            )
            sh, sm, sl = parts(stencil)
            columns.append(jnp.concatenate([sh, sh, sh, sm, sm, sl], axis=0))
        right = jnp.concatenate(columns, axis=1)
        out = jnp.dot(weights[...], right, preferred_element_type=jnp.float32)
        feat_ref[:, ny * LANE * x:ny * LANE * (x + 1)] = out.astype(jnp.bfloat16)
    f = feat_ref[...]
    gram_ref[...] = lax.dot_general(f, f, (((1,), (1,)), ((), ())), preferred_element_type=jnp.float32)


def front(fields, lo, hi, mix):
    nf, ns, nx, ny, nz = fields.shape
    width = ns * mix.shape[0]
    rows = 7 * nf * ns + 8
    return pl.pallas_call(
        functools.partial(front_kernel, (nf, ns, nx, ny)),
        out_shape=(
            jax.ShapeDtypeStruct((width, nx * ny * nz), jnp.bfloat16),
            jax.ShapeDtypeStruct((width, width), jnp.float32),
        ),
        in_specs=[pl.BlockSpec(memory_space=pltpu.VMEM)] * 4,
        out_specs=(pl.BlockSpec(memory_space=pltpu.VMEM),) * 2,
        scratch_shapes=[pltpu.VMEM((width, 6 * rows), jnp.bfloat16)],
        compiler_params=pltpu.CompilerParams(vmem_limit_bytes=48 << 20),
    )(fields.reshape(-1, nz), lo.reshape(-1, nz), hi.reshape(-1, nz), mix)


def running_kernel(
    side, steps, cells, gram_ref, out_ref,
    stack, pair_in, mine, got_a, got_b, got_y, whole,
    pair_send, pair_recv, a_send, a_recv, b_send, b_recv,
    y_send, y_recv, g_send, g_recv, f_send, f_recv,
):
    here = lax.axis_index("rows")
    t = lax.axis_index("tm")
    core = here % 2
    chip = here // 2
    z, x = chip // side, chip % side
    a = (1 - core) * x + core * z
    b = (1 - core) * z + core * x
    a_step = (1 - core) + core * side
    b_step = (1 - core) * side + core
    half = stack.shape[1]
    piece = half // side

    def at_a(k):
        return {"rows": 2 * (k * a_step + b * b_step) + core}

    def at_b(k):
        return {"rows": 2 * (a * a_step + k * b_step) + core}

    def at_t(k):
        return {"tm": k}

    partner = {"rows": 2 * chip + 1 - core}

    def copy(src, dst, send, recv, to):
        return pltpu.make_async_remote_copy(
            src_ref=src, dst_ref=dst, send_sem=send, recv_sem=recv,
            device_id=to, device_id_type=MESH,
        )

    barrier = pltpu.get_barrier_semaphore()
    pl.semaphore_signal(barrier, inc=1, device_id=partner, device_id_type=MESH)
    for d in range(1, side):
        pl.semaphore_signal(barrier, inc=1, device_id=at_a((a + d) % side), device_id_type=MESH)
        pl.semaphore_signal(barrier, inc=1, device_id=at_b((b + d) % side), device_id_type=MESH)
    for d in range(1, steps):
        pl.semaphore_signal(barrier, inc=1, device_id=at_t((t + d) % steps), device_id_type=MESH)

    edge = gram_ref.shape[0] // 2
    flat = [gram_ref[:edge, :edge], gram_ref[edge:, :edge], gram_ref[edge:, edge:]]
    cut = edge // 2
    stack[0, :edge] = flat[0]
    stack[0, edge:] = flat[1][:cut]
    stack[1, :cut] = flat[1][cut:]
    stack[1, cut:] = flat[2]

    pl.semaphore_wait(barrier, 2 * (side - 1) + steps)

    sends = []
    pair = copy(stack.at[1 - core], pair_in, pair_send, pair_recv, partner)
    pair.start()
    sends.append(pair)
    pair.wait_recv()
    mine[...] = (stack[core] + pair_in[...]).reshape(mine.shape)

    for d in range(1, side):
        k = (a + d) % side
        c = copy(mine.at[k], got_a.at[a], a_send.at[d], a_recv.at[a], at_a(k))
        c.start()
        sends.append(c)
    total = mine[a]
    for d in range(1, side):
        k = (a + d) % side
        copy(mine.at[a], got_a.at[k], a_send.at[d], a_recv.at[k], at_a(k)).wait_recv()
        total = total + got_a[k]
    got_b[b] = total

    for d in range(1, side):
        k = (b + d) % side
        c = copy(got_b.at[b], got_b.at[b], b_send.at[d], b_recv.at[b], at_b(k))
        c.start()
        sends.append(c)
    for d in range(1, side):
        k = (b + d) % side
        copy(got_b.at[b], got_b.at[k], b_send.at[d], b_recv.at[k], at_b(k)).wait_recv()
    total = got_b[0]
    for k in range(1, side):
        total = total + got_b[k]
    got_y[t] = total

    for d in range(1, steps):
        k = t + d

        @pl.when(k < steps)
        def _():
            copy(got_y.at[t], got_y.at[t], y_send.at[d], y_recv.at[t], at_t(k)).start()

    whole[core, a] = jnp.zeros_like(total)
    for k in range(steps):

        @pl.when(k < t)
        def _():
            copy(got_y.at[k], got_y.at[k], y_send.at[0], y_recv.at[k], at_t(k)).wait_recv()

        @pl.when(k <= t)
        def _():
            whole[core, a] += got_y[k]

    count = (t + 1).astype(jnp.float32) * jnp.float32(cells)
    whole[core, a] = whole[core, a] / count

    def forward(k):
        return copy(whole.at[core, k], whole.at[core, k], f_send.at[k], f_recv.at[k], partner)

    for d in range(1, side):
        k = (a + d) % side
        c = copy(whole.at[core, a], whole.at[core, a], g_send.at[d], g_recv.at[a], at_a(k))
        c.start()
        sends.append(c)
    c = forward(a)
    c.start()
    sends.append(c)
    for d in range(1, side):
        k = (a + d) % side
        copy(whole.at[core, a], whole.at[core, k], g_send.at[d], g_recv.at[k], at_a(k)).wait_recv()
        c = forward(k)
        c.start()
        sends.append(c)
    for k in range(side):
        copy(
            whole.at[core, k], whole.at[1 - core, k], f_send.at[k], f_recv.at[k], partner
        ).wait_recv()

    first = whole[0].reshape(half, edge)
    second = whole[1].reshape(half, edge)
    out_ref[:edge, :edge] = first[:edge]
    out_ref[edge:edge + cut, :edge] = first[edge:]
    out_ref[edge + cut:, :edge] = second[:cut]
    out_ref[edge:, edge:] = second[cut:]
    out_ref[:edge, edge:] = jnp.concatenate([first[edge:], second[:cut]], axis=0).T

    for c in sends:
        c.wait_send()
    for d in range(1, steps):
        k = t + d

        @pl.when(k < steps)
        def _():
            copy(got_y.at[t], got_y.at[t], y_send.at[d], y_recv.at[t], at_t(k)).wait_send()


def running_mean(gram, cells):
    side = math.isqrt(lax.axis_size("rows") // 2)
    steps = lax.axis_size("tm")
    width = gram.shape[0]
    edge = width // 2
    half = 3 * edge // 2
    piece = half // side
    dma = pltpu.SemaphoreType.DMA
    f32 = jnp.float32
    return pl.pallas_call(
        functools.partial(running_kernel, side, steps, cells * lax.axis_size("rows")),
        out_shape=jax.ShapeDtypeStruct((width, width), f32),
        in_specs=[pl.BlockSpec(memory_space=pltpu.VMEM)],
        out_specs=pl.BlockSpec(memory_space=pltpu.VMEM),
        scratch_shapes=[
            pltpu.VMEM((2, half, edge), f32),
            pltpu.VMEM((half, edge), f32),
            pltpu.VMEM((side, piece, edge), f32),
            pltpu.VMEM((side, piece, edge), f32),
            pltpu.VMEM((side, piece, edge), f32),
            pltpu.VMEM((steps, piece, edge), f32),
            pltpu.VMEM((2, side, piece, edge), f32),
            dma, dma,
            dma((side,)), dma((side,)),
            dma((side,)), dma((side,)),
            dma((steps,)), dma((steps,)),
            dma((side,)), dma((side,)),
            dma((side,)), dma((side,)),
        ],
        compiler_params=pltpu.CompilerParams(collective_id=0, has_side_effects=True),
    )(gram)


def body(fields, channel_mix):
    count = lax.axis_size("rows")
    up = [(i, i + 1) for i in range(count - 1)]
    down = [(i + 1, i) for i in range(count - 1)]
    lo = lax.ppermute(fields[:, :, -1:], "rows", up)
    hi = lax.ppermute(fields[:, :, :1], "rows", down)
    features, gram = front(fields, lo, hi, channel_mix)
    factor, solved = factor_and_solve(running_mean(gram, features.shape[1]), features)
    _, snaps, nx, ny, nz = fields.shape
    coefficients = solved.reshape(snaps, channel_mix.shape[0], nx, ny, nz)
    return (factor[None], coefficients)


def solution(mesh):
    return jax.shard_map(
        body,
        mesh=mesh,
        in_specs=(P(None, "tm", "rows", None, None), P()),
        out_specs=(P("tm", None, None), P("tm", None, "rows", None, None)),
        check_vma=False,
    )
```

```python
import functools
import math

import jax
import jax.numpy as jnp
from jax import lax
from jax.experimental import pallas as pl
from jax.experimental.pallas import tpu as pltpu
from jax.sharding import PartitionSpec as P

MESH = pl.DeviceIdType.MESH
ROW, LANE, PANEL = 8, 128, 32


def parts(v):
    high = v.astype(jnp.bfloat16)
    rest = v - high.astype(jnp.float32)
    mid = rest.astype(jnp.bfloat16)
    low = (rest - mid.astype(jnp.float32)).astype(jnp.bfloat16)
    return high, mid, low


def eliminate(rows, col0, tiles):
    sub = lax.broadcasted_iota(jnp.int32, (ROW, LANE), 0)
    count = len(rows)

    def spread(v, q):
        return jnp.broadcast_to(v[q:q + 1, :], (ROW, LANE))

    for k in range(count):
        lane = (col0 + ROW * k) % LANE
        tc = tiles.index((col0 + ROW * k) // LANE)
        cols = [
            [jnp.broadcast_to(rows[i][tc][:, lane + q:lane + q + 1], (ROW, LANE)) for i in range(k, count)]
            for q in range(ROW)
        ]
        scale = jnp.zeros((ROW, LANE), jnp.float32)
        for q in range(ROW):
            pivot = spread(cols[q][0], q)
            inv = 1.0 / pivot
            scale = jnp.where(sub == q, lax.rsqrt(pivot), scale)
            mult = [c * inv for c in cols[q]]
            mult[0] = jnp.where(sub > q, mult[0], 0.0)
            for p in range(q + 1, ROW):
                line = spread(cols[p][0], q)
                cols[p] = [c - m * line for c, m in zip(cols[p], mult)]
            for t in range(len(tiles)):
                line = spread(rows[k][t], q)
                for i, m in enumerate(mult):
                    rows[k + i][t] = rows[k + i][t] - m * line
        for t in range(len(tiles)):
            rows[k][t] = rows[k][t] * scale
    return rows


def factor_kernel(gram_ref, feat_ref, fac_ref, out_ref, work, spread_out):
    n = gram_ref.shape[0]
    steps = n // PANEL
    work[:, :n] = gram_ref[...]
    eye_r = lax.broadcasted_iota(jnp.int32, (n, n), 0)
    eye_c = lax.broadcasted_iota(jnp.int32, (n, n), 1)
    work[:, n:] = jnp.where(eye_r == eye_c, 1.0, 0.0)
    left = n // LANE
    for p in range(steps):
        r0 = PANEL * p
        first = r0 // LANE
        tiles = list(range(first, left + first + 1))
        rows = [
            [work[r0 + ROW * i:r0 + ROW * (i + 1), LANE * t:LANE * (t + 1)] for t in tiles]
            for i in range(PANEL // ROW)
        ]
        rows = eliminate(rows, r0, tiles)
        whole = jnp.concatenate([jnp.concatenate(r, axis=1) for r in rows], axis=0)
        wide = LANE * (left - first)
        upper = whole[:, :wide]
        rr = r0 + lax.broadcasted_iota(jnp.int32, (PANEL, wide), 0)
        cc = LANE * first + lax.broadcasted_iota(jnp.int32, (PANEL, wide), 1)
        upper = jnp.where(cc >= rr, upper, 0.0)
        lower = upper.T
        fac_ref[LANE * first:, r0:r0 + PANEL] = lower
        if first:
            fac_ref[:LANE * first, r0:r0 + PANEL] = jnp.zeros((LANE * first, PANEL), jnp.float32)
        work[r0:r0 + PANEL, n:n + LANE * (first + 1)] = whole[:, wide:]
        r1 = r0 + PANEL
        if r1 < n:
            high, mid, low = parts(whole)
            right = jnp.concatenate([high, high, high, mid, mid, low], axis=0)
            lh, lm, ll = parts(lower)
            lhs = jnp.concatenate([lh, lm, ll, lh, lm, lh], axis=1)
            off = LANE * first
            for s0, s1 in ((r1, r1 + PANEL), (r1 + PANEL, n)):
                if s0 < s1:
                    change = jnp.dot(lhs[s0 - off:s1 - off], right, preferred_element_type=jnp.float32)
                    at = LANE * tiles[0]
                    work[s0:s1, at:at + LANE * len(tiles)] -= change
    inverse = work[:, n:]
    high = inverse.astype(jnp.bfloat16)
    mid = (inverse - high.astype(jnp.float32)).astype(jnp.bfloat16)
    cells = feat_ref.shape[1]
    blocks = cells // LANE
    chunk = 4
    for j in range(blocks // chunk):
        x = feat_ref[:, chunk * LANE * j:chunk * LANE * (j + 1)]
        y = jnp.dot(high, x, preferred_element_type=jnp.float32)
        y = y + jnp.dot(mid, x, preferred_element_type=jnp.float32)
        for b in range(chunk):
            spread_out[pl.ds(j * chunk + b, n, stride=blocks), :] = y[:, LANE * b:LANE * (b + 1)]
    out_ref[...] = spread_out[...].astype(jnp.bfloat16)


def factor_and_solve(gram, features):
    n, cells = features.shape
    lines = n * cells // LANE
    return pl.pallas_call(
        factor_kernel,
        out_shape=(
            jax.ShapeDtypeStruct((n, n), jnp.float32),
            jax.ShapeDtypeStruct((lines, LANE), jnp.bfloat16),
        ),
        in_specs=[pl.BlockSpec(memory_space=pltpu.VMEM)] * 2,
        out_specs=(pl.BlockSpec(memory_space=pltpu.VMEM),) * 2,
        scratch_shapes=[
            pltpu.VMEM((n, 2 * n), jnp.float32),
            pltpu.VMEM((lines, LANE), jnp.float32),
        ],
        compiler_params=pltpu.CompilerParams(vmem_limit_bytes=48 << 20),
    )(gram, features)


def spread_mix(mix, snaps, fields, rows):
    ch, count = mix.shape
    group = fields * snaps
    stencils = count // fields
    k = lax.broadcasted_iota(jnp.int32, (count, rows), 0)
    col = lax.broadcasted_iota(jnp.int32, (count, rows), 1)
    pick = (k // stencils == col % group // snaps) & (k % stencils == col // group)
    pick = jnp.where(pick, 1.0, 0.0).astype(jnp.bfloat16)
    r = lax.broadcasted_iota(jnp.int32, (snaps * ch, rows), 0)
    c = lax.broadcasted_iota(jnp.int32, (snaps * ch, rows), 1)
    same = r // ch == c % snaps
    out = []
    for part in parts(mix):
        wide = jnp.dot(part, pick, preferred_element_type=jnp.float32)
        wide = jnp.concatenate([wide] * snaps, axis=0)
        out.append(jnp.where(same, wide, 0.0).astype(jnp.bfloat16))
    return out


def gram_kernel(
    dims, side, steps, count, u_hbm, mix_ref, feat_hbm, out_ref,
    u_ref, feat, weights, to_left, to_right, lo, hi,
    stack, pair_in, mine, got_a, got_b, got_y, whole,
    u_sem, feat_sem, l_send, l_recv, r_send, r_recv,
    pair_send, pair_recv, a_send, a_recv, b_send, b_recv,
    y_send, y_recv, g_send, g_recv, f_send, f_recv,
):
    fields, snaps, nx, ny = dims
    fs = fields * snaps
    load = pltpu.make_async_copy(u_hbm, u_ref, u_sem)
    load.start()
    here = lax.axis_index("rows")
    t = lax.axis_index("tm")
    size = 2 * side * side
    core = here % 2
    chip = here // 2
    z, x = chip // side, chip % side
    a = (1 - core) * x + core * z
    b = (1 - core) * z + core * x
    a_step = (1 - core) + core * side
    b_step = (1 - core) * side + core
    half = stack.shape[1]
    piece = half // side

    def at_a(k):
        return {"rows": 2 * (k * a_step + b * b_step) + core}

    def at_b(k):
        return {"rows": 2 * (a * a_step + k * b_step) + core}

    def at_t(k):
        return {"tm": k}

    partner = {"rows": 2 * chip + 1 - core}

    def copy(src, dst, send, recv, to):
        return pltpu.make_async_remote_copy(
            src_ref=src, dst_ref=dst, send_sem=send, recv_sem=recv,
            device_id=to, device_id_type=MESH,
        )

    left = {"rows": (here + size - 1) % size}
    right = {"rows": (here + 1) % size}
    barrier = pltpu.get_barrier_semaphore()
    for near in (left, right, partner):
        pl.semaphore_signal(barrier, inc=1, device_id=near, device_id_type=MESH)
    for d in range(1, side):
        pl.semaphore_signal(barrier, inc=1, device_id=at_a((a + d) % side), device_id_type=MESH)
        pl.semaphore_signal(barrier, inc=1, device_id=at_b((b + d) % side), device_id_type=MESH)
    for d in range(1, steps):
        pl.semaphore_signal(barrier, inc=1, device_id=at_t((t + d) % steps), device_id_type=MESH)

    rows = 7 * fs + 8
    h, m, l = spread_mix(mix_ref[...], snaps, fields, rows)
    for i, w in enumerate((h, m, l, h, m, h)):
        weights[:, rows * i:rows * (i + 1)] = w

    def at(x, y):
        return u_ref[pl.ds(x * ny + y, fs, stride=nx * ny), :]

    load.wait()
    for y in range(ny):
        to_left[fs * y:fs * (y + 1), :] = at(0, y)
        to_right[fs * y:fs * (y + 1), :] = at(nx - 1, y)

    pl.semaphore_wait(barrier, 2 * (side - 1) + steps + 2)

    go_left = copy(to_left, hi, l_send, l_recv, left)
    go_right = copy(to_right, lo, r_send, r_recv, right)
    go_left.start()
    go_right.start()
    sends = [go_left, go_right]

    lane = lax.broadcasted_iota(jnp.int32, (fs, LANE), 1)
    zero = jnp.zeros((fs, LANE), jnp.float32)
    pad = jnp.zeros((8, LANE), jnp.float32)

    def plane(x, before, after):
        mid = [at(x, y) for y in range(ny)]
        columns = []
        for y in range(ny):
            u = mid[y]
            xp, xm = after(y), before(y)
            yp = mid[y + 1] if y + 1 < ny else zero
            ym = mid[y - 1] if y else zero
            zp = jnp.where(lane == LANE - 1, 0.0, pltpu.roll(u, LANE - 1, 1))
            zm = jnp.where(lane == 0, 0.0, pltpu.roll(u, 1, 1))
            twice = 2.0 * u
            stencil = jnp.concatenate(
                [
                    u,
                    0.5 * (xp - xm), 0.5 * (yp - ym), 0.5 * (zp - zm),
                    0.25 * (xp - twice + xm), 0.25 * (yp - twice + ym), 0.25 * (zp - twice + zm),
                    pad,
                ],
                axis=0,
            )
            sh, sm, sl = parts(stencil)
            columns.append(jnp.concatenate([sh, sh, sh, sm, sm, sl], axis=0))
        values = jnp.dot(weights[...], jnp.concatenate(columns, axis=1), preferred_element_type=jnp.float32)
        feat[:, ny * LANE * x:ny * LANE * (x + 1)] = values.astype(jnp.bfloat16)

    for x in range(1, nx - 1):
        plane(x, lambda y: at(x - 1, y), lambda y: at(x + 1, y))

    go_right.wait_recv()
    plane(
        0,
        lambda y: jnp.where(here > 0, lo[fs * y:fs * (y + 1), :], 0.0),
        lambda y: at(1, y),
    )
    go_left.wait_recv()
    plane(
        nx - 1,
        lambda y: at(nx - 2, y),
        lambda y: jnp.where(here < size - 1, hi[fs * y:fs * (y + 1), :], 0.0),
    )

    keep = pltpu.make_async_copy(feat, feat_hbm, feat_sem)
    keep.start()
    edge = out_ref.shape[0] // 2
    cut = edge // 2
    f = feat[...]
    gram = lax.dot_general(f, f, (((1,), (1,)), ((), ())), preferred_element_type=jnp.float32)
    stack[0, :edge] = gram[:edge, :edge]
    stack[0, edge:] = gram[edge:edge + cut, :edge]
    stack[1, :cut] = gram[edge + cut:, :edge]
    stack[1, cut:] = gram[edge:, edge:]

    pair = copy(stack.at[1 - core], pair_in, pair_send, pair_recv, partner)
    pair.start()
    sends.append(pair)
    pair.wait_recv()
    mine[...] = (stack[core] + pair_in[...]).reshape(mine.shape)

    for d in range(1, side):
        k = (a + d) % side
        c = copy(mine.at[k], got_a.at[a], a_send.at[d], a_recv.at[a], at_a(k))
        c.start()
        sends.append(c)
    total = mine[a]
    for d in range(1, side):
        k = (a + d) % side
        copy(mine.at[a], got_a.at[k], a_send.at[d], a_recv.at[k], at_a(k)).wait_recv()
        total = total + got_a[k]
    got_b[b] = total

    for d in range(1, side):
        k = (b + d) % side
        c = copy(got_b.at[b], got_b.at[b], b_send.at[d], b_recv.at[b], at_b(k))
        c.start()
        sends.append(c)
    for d in range(1, side):
        k = (b + d) % side
        copy(got_b.at[b], got_b.at[k], b_send.at[d], b_recv.at[k], at_b(k)).wait_recv()
    total = got_b[0]
    for k in range(1, side):
        total = total + got_b[k]
    got_y[t] = total

    for d in range(1, steps):
        k = t + d

        @pl.when(k < steps)
        def _():
            copy(got_y.at[t], got_y.at[t], y_send.at[d], y_recv.at[t], at_t(k)).start()

    whole[core, a] = jnp.zeros_like(total)
    for k in range(steps):

        @pl.when(k < t)
        def _():
            copy(got_y.at[k], got_y.at[k], y_send.at[0], y_recv.at[k], at_t(k)).wait_recv()

        @pl.when(k <= t)
        def _():
            whole[core, a] += got_y[k]

    whole[core, a] = whole[core, a] / ((t + 1).astype(jnp.float32) * jnp.float32(count))

    def forward(k):
        return copy(whole.at[core, k], whole.at[core, k], f_send.at[k], f_recv.at[k], partner)

    for d in range(1, side):
        k = (a + d) % side
        c = copy(whole.at[core, a], whole.at[core, a], g_send.at[d], g_recv.at[a], at_a(k))
        c.start()
        sends.append(c)
    c = forward(a)
    c.start()
    sends.append(c)
    for d in range(1, side):
        k = (a + d) % side
        copy(whole.at[core, a], whole.at[core, k], g_send.at[d], g_recv.at[k], at_a(k)).wait_recv()
        c = forward(k)
        c.start()
        sends.append(c)
    for k in range(side):
        copy(
            whole.at[core, k], whole.at[1 - core, k], f_send.at[k], f_recv.at[k], partner
        ).wait_recv()

    first = whole[0].reshape(half, edge)
    second = whole[1].reshape(half, edge)
    out_ref[:edge, :edge] = first[:edge]
    out_ref[edge:edge + cut, :edge] = first[edge:]
    out_ref[edge + cut:, :edge] = second[:cut]
    out_ref[edge:, edge:] = second[cut:]
    out_ref[:edge, edge:] = jnp.concatenate([first[edge:], second[:cut]], axis=0).T

    for c in sends:
        c.wait_send()
    for d in range(1, steps):
        k = t + d

        @pl.when(k < steps)
        def _():
            copy(got_y.at[t], got_y.at[t], y_send.at[d], y_recv.at[t], at_t(k)).wait_send()
    keep.wait()


def features_and_mean(fields, mix):
    nf, ns, nx, ny, nz = fields.shape
    side = math.isqrt(lax.axis_size("rows") // 2)
    steps = lax.axis_size("tm")
    width = ns * mix.shape[0]
    cells = nx * ny * nz
    rows = 7 * nf * ns + 8
    edge = width // 2
    half = 3 * edge // 2
    piece = half // side
    plane = nf * ns * ny
    dma = pltpu.SemaphoreType.DMA
    f32, bf16 = jnp.float32, jnp.bfloat16
    return pl.pallas_call(
        functools.partial(gram_kernel, (nf, ns, nx, ny), side, steps, cells * lax.axis_size("rows")),
        out_shape=(jax.ShapeDtypeStruct((width, cells), bf16), jax.ShapeDtypeStruct((width, width), f32)),
        in_specs=[pl.BlockSpec(memory_space=pl.ANY), pl.BlockSpec(memory_space=pltpu.VMEM)],
        out_specs=(pl.BlockSpec(memory_space=pl.ANY), pl.BlockSpec(memory_space=pltpu.VMEM)),
        scratch_shapes=[
            pltpu.VMEM((nf * ns * nx * ny, nz), f32),
            pltpu.VMEM((width, cells), bf16),
            pltpu.VMEM((width, 6 * rows), bf16),
            pltpu.VMEM((plane, nz), f32),
            pltpu.VMEM((plane, nz), f32),
            pltpu.VMEM((plane, nz), f32),
            pltpu.VMEM((plane, nz), f32),
            pltpu.VMEM((2, half, edge), f32),
            pltpu.VMEM((half, edge), f32),
            pltpu.VMEM((side, piece, edge), f32),
            pltpu.VMEM((side, piece, edge), f32),
            pltpu.VMEM((side, piece, edge), f32),
            pltpu.VMEM((steps, piece, edge), f32),
            pltpu.VMEM((2, side, piece, edge), f32),
            dma, dma, dma, dma, dma, dma,
            dma, dma,
            dma((side,)), dma((side,)),
            dma((side,)), dma((side,)),
            dma((steps,)), dma((steps,)),
            dma((side,)), dma((side,)),
            dma((side,)), dma((side,)),
        ],
        compiler_params=pltpu.CompilerParams(
            collective_id=0, has_side_effects=True, vmem_limit_bytes=56 << 20
        ),
    )(fields.reshape(-1, nz), mix)


def body(fields, channel_mix):
    features, mean = features_and_mean(fields, channel_mix)
    factor, solved = factor_and_solve(mean, features)
    _, snaps, nx, ny, nz = fields.shape
    coefficients = solved.reshape(snaps, channel_mix.shape[0], nx, ny, nz)
    return (factor[None], coefficients)


def solution(mesh):
    return jax.shard_map(
        body,
        mesh=mesh,
        in_specs=(P(None, "tm", "rows", None, None), P()),
        out_specs=(P("tm", None, None), P("tm", None, "rows", None, None)),
        check_vma=False,
    )
```

```python
import functools
import math

import jax
import jax.numpy as jnp
from jax import lax
from jax.experimental import pallas as pl
from jax.experimental.pallas import tpu as pltpu
from jax.sharding import PartitionSpec as P

MESH = pl.DeviceIdType.MESH
ROW, LANE, PANEL = 8, 128, 32
PITCH = 40


def parts(v):
    high = v.astype(jnp.bfloat16)
    rest = v - high.astype(jnp.float32)
    mid = rest.astype(jnp.bfloat16)
    low = (rest - mid.astype(jnp.float32)).astype(jnp.bfloat16)
    return high, mid, low


def eliminate(rows, col0, tiles):
    sub = lax.broadcasted_iota(jnp.int32, (ROW, LANE), 0)
    count = len(rows)

    def spread(v, q):
        return jnp.broadcast_to(v[q:q + 1, :], (ROW, LANE))

    for k in range(count):
        lane = (col0 + ROW * k) % LANE
        tc = tiles.index((col0 + ROW * k) // LANE)
        cols = [
            [jnp.broadcast_to(rows[i][tc][:, lane + q:lane + q + 1], (ROW, LANE)) for i in range(k, count)]
            for q in range(ROW)
        ]
        scale = jnp.zeros((ROW, LANE), jnp.float32)
        for q in range(0, ROW, 2):
            p0, cross, p1 = spread(cols[q][0], q), spread(cols[q][0], q + 1), spread(cols[q + 1][0], q + 1)
            det = p0 * p1 - cross * cross
            inv0 = 1.0 / p0
            inv1 = p0 * (1.0 / det)
            ratio = cross * inv0
            scale = jnp.where(sub == q, lax.rsqrt(p0), scale)
            scale = jnp.where(sub == q + 1, lax.rsqrt(det * inv0), scale)
            m0 = [c * inv0 for c in cols[q]]
            m0[0] = jnp.where(sub > q, m0[0], 0.0)
            m1 = [(c - m * cross) * inv1 for c, m in zip(cols[q + 1], m0)]
            m1[0] = jnp.where(sub > q + 1, m1[0], 0.0)
            for p in range(q + 2, ROW):
                line0 = spread(cols[p][0], q)
                line1 = spread(cols[p][0], q + 1) - ratio * line0
                cols[p] = [(c - a * line0) - b * line1 for c, a, b in zip(cols[p], m0, m1)]
            for t in range(len(tiles)):
                line0 = spread(rows[k][t], q)
                line1 = spread(rows[k][t], q + 1) - ratio * line0
                for i in range(len(m0)):
                    rows[k + i][t] = (rows[k + i][t] - m0[i] * line0) - m1[i] * line1
        for t in range(len(tiles)):
            rows[k][t] = rows[k][t] * scale
    return rows


def factor_kernel(
    mean_hbm, feat_hbm, fac_ref, out_hbm, mean, work, feat, spread_out, packed, mean_sem, feat_sem, out_sems
):
    n = work.shape[0]
    steps = n // PANEL
    top = n // 2
    load = pltpu.make_async_copy(mean_hbm, mean, mean_sem)
    load.start()
    fetch = pltpu.make_async_copy(feat_hbm, feat, feat_sem)
    fetch.start()
    eye_r = lax.broadcasted_iota(jnp.int32, (n, n), 0)
    eye_c = lax.broadcasted_iota(jnp.int32, (n, n), 1)
    work[:, n:] = jnp.where(eye_r == eye_c, 1.0, 0.0)
    left = n // LANE
    blocks = feat.shape[1] // LANE
    stores = []

    def apply(r0, r1, depth):
        count = r1 - r0
        inverse = work[r0:r1, n:n + depth]
        high = inverse.astype(jnp.bfloat16)
        mid = (inverse - high.astype(jnp.float32)).astype(jnp.bfloat16)
        both = jnp.concatenate([high, mid], axis=0)
        chunk = 4
        for j in range(blocks // chunk):
            x = feat[:depth, chunk * LANE * j:chunk * LANE * (j + 1)]
            y = jnp.dot(both, x, preferred_element_type=jnp.float32)
            y = y[:count] + y[count:]
            for b in range(chunk):
                spread_out[pl.ds(r0 * PITCH + j * chunk + b, count, stride=PITCH), :] = y[:, LANE * b:LANE * (b + 1)]
        lines = pl.ds(r0 * blocks, count * blocks)
        wide = spread_out[pl.ds(r0 * PITCH, count * PITCH), :].reshape(count, PITCH, LANE)[:, :blocks]
        packed[lines, :] = wide.reshape(count * blocks, LANE).astype(jnp.bfloat16)
        c = pltpu.make_async_copy(packed.at[lines], out_hbm.at[lines], out_sems.at[len(stores)])
        c.start()
        stores.append(c)

    load.wait()
    parts_of = [mean[h, k] for h in range(2) for k in range(mean.shape[1])]
    e = (mean.shape[2] - 1) // 2
    cross = jnp.concatenate([v[:e] for v in parts_of], axis=0)
    mixed = jnp.concatenate([v[e:2 * e] for v in parts_of], axis=0)
    line = sum(v[2 * e:] for v in parts_of[1:]) + parts_of[0][2 * e:]
    er = lax.broadcasted_iota(jnp.int32, (top, top), 0)
    ec = lax.broadcasted_iota(jnp.int32, (top, top), 1)
    turned = mixed.T
    work[:top, :top] = jnp.where(er >= ec, mixed, turned)
    work[:top, top:n] = cross.T
    work[top:, :top] = cross
    work[top:, top:n] = jnp.where(er == ec, line, jnp.where(ec > er, mixed, turned))
    for p in range(steps):
        r0 = PANEL * p
        first = r0 // LANE
        tiles = list(range(first, left + first + 1))
        rows = [
            [work[r0 + ROW * i:r0 + ROW * (i + 1), LANE * t:LANE * (t + 1)] for t in tiles]
            for i in range(PANEL // ROW)
        ]
        rows = eliminate(rows, r0, tiles)
        whole = jnp.concatenate([jnp.concatenate(r, axis=1) for r in rows], axis=0)
        wide = LANE * (left - first)
        upper = whole[:, :wide]
        rr = r0 + lax.broadcasted_iota(jnp.int32, (PANEL, wide), 0)
        cc = LANE * first + lax.broadcasted_iota(jnp.int32, (PANEL, wide), 1)
        upper = jnp.where(cc >= rr, upper, 0.0)
        lower = upper.T
        fac_ref[LANE * first:, r0:r0 + PANEL] = lower
        if first:
            fac_ref[:LANE * first, r0:r0 + PANEL] = jnp.zeros((LANE * first, PANEL), jnp.float32)
        work[r0:r0 + PANEL, n:n + LANE * (first + 1)] = whole[:, wide:]
        r1 = r0 + PANEL
        if r1 < n:
            high, mid, low = parts(whole)
            right = jnp.concatenate([high, high, high, mid, mid, low], axis=0)
            lh, lm, ll = parts(upper)
            lhs = jnp.concatenate([lh, lm, ll, lh, lm, lh], axis=0).T
            off = LANE * first
            for s0, s1 in ((r1, r1 + PANEL), (r1 + PANEL, n)):
                if s0 < s1:
                    change = jnp.dot(lhs[s0 - off:s1 - off], right, preferred_element_type=jnp.float32)
                    at = LANE * tiles[0]
                    work[s0:s1, at:at + LANE * len(tiles)] -= change
        if p == top // PANEL - 1:
            fetch.wait()
        if p >= top // PANEL and p < steps - 1:
            part = {4: (0, 32), 5: (32, 64), 6: (64, 128)}[p]
            apply(part[0], part[1], top)
    for r0 in range(top, n, n // 4):
        apply(r0, r0 + n // 4, n)
    for c in stores:
        c.wait()


def factor_and_solve(mean, features):
    n, cells = features.shape
    lines = n * cells // LANE
    dma = pltpu.SemaphoreType.DMA
    return pl.pallas_call(
        factor_kernel,
        out_shape=(
            jax.ShapeDtypeStruct((n, n), jnp.float32),
            jax.ShapeDtypeStruct((lines, LANE), jnp.bfloat16),
        ),
        in_specs=[pl.BlockSpec(memory_space=pl.ANY)] * 2,
        out_specs=(pl.BlockSpec(memory_space=pltpu.VMEM), pl.BlockSpec(memory_space=pl.ANY)),
        scratch_shapes=[
            pltpu.VMEM(mean.shape, jnp.float32),
            pltpu.VMEM((n, 2 * n), jnp.float32),
            pltpu.VMEM((n, cells), jnp.bfloat16),
            pltpu.VMEM((n * PITCH, LANE), jnp.float32),
            pltpu.VMEM((lines, LANE), jnp.bfloat16),
            dma, dma, dma((8,)),
        ],
        compiler_params=pltpu.CompilerParams(vmem_limit_bytes=62 << 20),
    )(mean, features)


def spread_mix(mix, snaps, fields, rows):
    ch, count = mix.shape
    group = fields * snaps
    stencils = count // fields
    k = lax.broadcasted_iota(jnp.int32, (count, rows), 0)
    col = lax.broadcasted_iota(jnp.int32, (count, rows), 1)
    pick = (k // stencils == col % group // snaps) & (k % stencils == col // group)
    pick = jnp.where(pick, 1.0, 0.0).astype(jnp.bfloat16)
    r = lax.broadcasted_iota(jnp.int32, (snaps * ch, rows), 0)
    c = lax.broadcasted_iota(jnp.int32, (snaps * ch, rows), 1)
    same = r // ch == c % snaps
    out = []
    for part in parts(mix):
        wide = jnp.dot(part, pick, preferred_element_type=jnp.float32)
        wide = jnp.concatenate([wide] * snaps, axis=0)
        out.append(jnp.where(same, wide, 0.0).astype(jnp.bfloat16))
    return out


def gram_kernel(
    dims, side, steps, count, u_hbm, mix_ref, feat_hbm, out_hbm,
    u_ref, cells, feat, weights, lo, hi,
    stack, pair_in, mine, got_a, got_b, got_y, whole,
    u_sem, feat_sem, out_sem, l_send, l_recv, r_send, r_recv,
    pair_send, pair_recv, a_send, a_recv, b_send, b_recv,
    y_send, y_recv, g_send, g_recv, f_send, f_recv,
):
    fields, snaps, nx, ny = dims
    fs = fields * snaps
    load = pltpu.make_async_copy(u_hbm, u_ref, u_sem)
    load.start()
    here = lax.axis_index("rows")
    t = lax.axis_index("tm")
    size = 2 * side * side
    core = here % 2
    chip = here // 2
    z, x = chip // side, chip % side
    a = (1 - core) * x + core * z
    b = (1 - core) * z + core * x
    a_step = (1 - core) + core * side
    b_step = (1 - core) * side + core
    far = sorted(range(1, side), key=lambda d: -min(d, side - d))
    far_t = sorted(range(1, steps), key=lambda d: -min(d, steps - d))

    def at_a(k):
        return {"rows": 2 * (k * a_step + b * b_step) + core}

    def at_b(k):
        return {"rows": 2 * (a * a_step + k * b_step) + core}

    def at_t(k):
        return {"tm": k}

    partner = {"rows": 2 * chip + 1 - core}

    def copy(src, dst, send, recv, to):
        return pltpu.make_async_remote_copy(
            src_ref=src, dst_ref=dst, send_sem=send, recv_sem=recv,
            device_id=to, device_id_type=MESH,
        )

    left = {"rows": (here + size - 1) % size}
    right = {"rows": (here + 1) % size}
    barrier = pltpu.get_barrier_semaphore()
    for near in (left, right, partner):
        pl.semaphore_signal(barrier, inc=1, device_id=near, device_id_type=MESH)
    for d in range(1, side):
        pl.semaphore_signal(barrier, inc=1, device_id=at_a((a + d) % side), device_id_type=MESH)
        pl.semaphore_signal(barrier, inc=1, device_id=at_b((b + d) % side), device_id_type=MESH)
    for d in range(1, steps):
        pl.semaphore_signal(barrier, inc=1, device_id=at_t((t + d) % steps), device_id_type=MESH)

    rows = 7 * fs + 8
    h, m, l = spread_mix(mix_ref[...], snaps, fields, rows)
    for i, w in enumerate((h, m, l, h, m, h)):
        weights[:, rows * i:rows * (i + 1)] = w

    def at(x, y):
        j = x * ny + y
        return cells[fs * j:fs * (j + 1), :]

    load.wait()
    for j in range(nx * ny):
        cells[fs * j:fs * (j + 1), :] = u_ref[pl.ds(j, fs, stride=nx * ny), :]

    lane = lax.broadcasted_iota(jnp.int32, (fs, LANE), 1)
    zero = jnp.zeros((fs, LANE), jnp.float32)
    pad = jnp.zeros((8, LANE), jnp.float32)

    def plane(x, before, after):
        mid = [at(x, y) for y in range(ny)]
        columns = []
        for y in range(ny):
            u = mid[y]
            xp, xm = after(y), before(y)
            yp = mid[y + 1] if y + 1 < ny else zero
            ym = mid[y - 1] if y else zero
            zp = jnp.where(lane == LANE - 1, 0.0, pltpu.roll(u, LANE - 1, 1))
            zm = jnp.where(lane == 0, 0.0, pltpu.roll(u, 1, 1))
            twice = 2.0 * u
            stencil = jnp.concatenate(
                [
                    u,
                    0.5 * (xp - xm), 0.5 * (yp - ym), 0.5 * (zp - zm),
                    0.25 * (xp - twice + xm), 0.25 * (yp - twice + ym), 0.25 * (zp - twice + zm),
                    pad,
                ],
                axis=0,
            )
            sh, sm, sl = parts(stencil)
            columns.append(jnp.concatenate([sh, sh, sh, sm, sm, sl], axis=0))
        values = jnp.dot(weights[...], jnp.concatenate(columns, axis=1), preferred_element_type=jnp.float32)
        feat[:, ny * LANE * x:ny * LANE * (x + 1)] = values.astype(jnp.bfloat16)

    ahead = 2
    for x in range(1, 1 + ahead):
        plane(x, lambda y: at(x - 1, y), lambda y: at(x + 1, y))

    pl.semaphore_wait(barrier, 2 * (side - 1) + steps + 2)

    block = fs * ny
    go_left = copy(cells.at[pl.ds(0, block)], hi, l_send, l_recv, left)
    go_right = copy(cells.at[pl.ds(block * (nx - 1), block)], lo, r_send, r_recv, right)
    go_left.start()
    go_right.start()
    sends = [go_left, go_right]

    for x in range(1 + ahead, nx - 1):
        plane(x, lambda y: at(x - 1, y), lambda y: at(x + 1, y))

    go_right.wait_recv()
    plane(
        0,
        lambda y: jnp.where(here > 0, lo[fs * y:fs * (y + 1), :], 0.0),
        lambda y: at(1, y),
    )
    go_left.wait_recv()
    plane(
        nx - 1,
        lambda y: at(nx - 2, y),
        lambda y: jnp.where(here < size - 1, hi[fs * y:fs * (y + 1), :], 0.0),
    )

    keep = pltpu.make_async_copy(feat, feat_hbm, feat_sem)
    keep.start()
    f = feat[...]
    gram = lax.dot_general(f, f, (((1,), (1,)), ((), ())), preferred_element_type=jnp.float32)
    edge = gram.shape[0] // 2
    e = (stack.shape[2] - 1) // 2
    er = lax.broadcasted_iota(jnp.int32, (edge, edge), 0)
    ec = lax.broadcasted_iota(jnp.int32, (edge, edge), 1)
    second = gram[edge:, edge:]
    mixed = jnp.where(er >= ec, gram[:edge, :edge], second)
    line = jnp.sum(jnp.where(er == ec, second, 0.0), axis=0, keepdims=True)
    owner = lax.broadcasted_iota(jnp.int32, (1, edge), 1) // e
    for i in range(2 * side):
        stack[i // side, i % side, :e] = gram[edge + e * i:edge + e * (i + 1), :edge]
        stack[i // side, i % side, e:2 * e] = mixed[e * i:e * (i + 1)]
        stack[i // side, i % side, 2 * e:] = jnp.where(owner == i, line, 0.0)

    pair = copy(stack.at[1 - core], pair_in, pair_send, pair_recv, partner)
    pair.start()
    sends.append(pair)
    pair.wait_recv()
    mine[...] = stack[core] + pair_in[...]

    for d in far:
        k = (a + d) % side
        c = copy(mine.at[k], got_a.at[a], a_send.at[d], a_recv.at[a], at_a(k))
        c.start()
        sends.append(c)
    total = mine[a]
    for d in far[::-1]:
        k = (a + d) % side
        copy(mine.at[a], got_a.at[k], a_send.at[d], a_recv.at[k], at_a(k)).wait_recv()
        total = total + got_a[k]
    got_b[b] = total

    for d in far:
        k = (b + d) % side
        c = copy(got_b.at[b], got_b.at[b], b_send.at[d], b_recv.at[b], at_b(k))
        c.start()
        sends.append(c)
    for d in far[::-1]:
        k = (b + d) % side
        copy(got_b.at[b], got_b.at[k], b_send.at[d], b_recv.at[k], at_b(k)).wait_recv()
    total = got_b[0]
    for k in range(1, side):
        total = total + got_b[k]
    got_y[t] = total

    for d in far_t:
        k = t + d

        @pl.when(k < steps)
        def _():
            copy(got_y.at[t], got_y.at[t], y_send.at[d], y_recv.at[t], at_t(k)).start()

    whole[core, a] = jnp.zeros_like(total)
    for k in range(steps):

        @pl.when(k < t)
        def _():
            copy(got_y.at[k], got_y.at[k], y_send.at[0], y_recv.at[k], at_t(k)).wait_recv()

        @pl.when(k <= t)
        def _():
            whole[core, a] += got_y[k]

    whole[core, a] = whole[core, a] / ((t + 1).astype(jnp.float32) * jnp.float32(count))

    def forward(k):
        return copy(whole.at[core, k], whole.at[core, k], f_send.at[k], f_recv.at[k], partner)

    for d in far:
        k = (a + d) % side
        c = copy(whole.at[core, a], whole.at[core, a], g_send.at[d], g_recv.at[a], at_a(k))
        c.start()
        sends.append(c)
    c = forward(a)
    c.start()
    sends.append(c)
    for d in far[::-1]:
        k = (a + d) % side
        copy(whole.at[core, a], whole.at[core, k], g_send.at[d], g_recv.at[k], at_a(k)).wait_recv()
        c = forward(k)
        c.start()
        sends.append(c)
    for k in range(side):
        copy(
            whole.at[core, k], whole.at[1 - core, k], f_send.at[k], f_recv.at[k], partner
        ).wait_recv()

    give = pltpu.make_async_copy(whole, out_hbm, out_sem)
    give.start()
    for c in sends:
        c.wait_send()
    for d in range(1, steps):
        k = t + d

        @pl.when(k < steps)
        def _():
            copy(got_y.at[t], got_y.at[t], y_send.at[d], y_recv.at[t], at_t(k)).wait_send()
    keep.wait()
    give.wait()


def features_and_mean(fields, mix):
    nf, ns, nx, ny, nz = fields.shape
    side = math.isqrt(lax.axis_size("rows") // 2)
    steps = lax.axis_size("tm")
    width = ns * mix.shape[0]
    cells = nx * ny * nz
    rows = 7 * nf * ns + 8
    edge = width // 2
    piece = (side, 2 * (edge // (2 * side)) + 1, edge)
    plane = nf * ns * ny
    dma = pltpu.SemaphoreType.DMA
    f32, bf16 = jnp.float32, jnp.bfloat16
    return pl.pallas_call(
        functools.partial(gram_kernel, (nf, ns, nx, ny), side, steps, cells * lax.axis_size("rows")),
        out_shape=(jax.ShapeDtypeStruct((width, cells), bf16), jax.ShapeDtypeStruct((2,) + piece, f32)),
        in_specs=[pl.BlockSpec(memory_space=pl.ANY), pl.BlockSpec(memory_space=pltpu.VMEM)],
        out_specs=(pl.BlockSpec(memory_space=pl.ANY),) * 2,
        scratch_shapes=[
            pltpu.VMEM((nf * ns * nx * ny, nz), f32),
            pltpu.VMEM((nf * ns * nx * ny, nz), f32),
            pltpu.VMEM((width, cells), bf16),
            pltpu.VMEM((width, 6 * rows), bf16),
            pltpu.VMEM((plane, nz), f32),
            pltpu.VMEM((plane, nz), f32),
            pltpu.VMEM((2,) + piece, f32),
            pltpu.VMEM(piece, f32),
            pltpu.VMEM(piece, f32),
            pltpu.VMEM(piece, f32),
            pltpu.VMEM(piece, f32),
            pltpu.VMEM((steps,) + piece[1:], f32),
            pltpu.VMEM((2,) + piece, f32),
            dma, dma, dma, dma, dma, dma, dma,
            dma, dma,
            dma((side,)), dma((side,)),
            dma((side,)), dma((side,)),
            dma((steps,)), dma((steps,)),
            dma((side,)), dma((side,)),
            dma((side,)), dma((side,)),
        ],
        compiler_params=pltpu.CompilerParams(
            collective_id=0, has_side_effects=True, vmem_limit_bytes=56 << 20
        ),
    )(fields.reshape(-1, nz), mix)


def body(fields, channel_mix):
    features, mean = features_and_mean(fields, channel_mix)
    factor, solved = factor_and_solve(mean, features)
    _, snaps, nx, ny, nz = fields.shape
    coefficients = solved.reshape(snaps, channel_mix.shape[0], nx, ny, nz)
    return (factor[None], coefficients)


def solution(mesh):
    return jax.shard_map(
        body,
        mesh=mesh,
        in_specs=(P(None, "tm", "rows", None, None), P()),
        out_specs=(P("tm", None, None), P("tm", None, "rows", None, None)),
        check_vma=False,
    )
```

```python
import functools
import math

import jax
import jax.numpy as jnp
from jax import lax
from jax.experimental import pallas as pl
from jax.experimental.pallas import tpu as pltpu
from jax.sharding import PartitionSpec as P

MESH = pl.DeviceIdType.MESH
ROW, LANE, PANEL = 8, 128, 32
PITCH = 40


def parts(v):
    high = v.astype(jnp.bfloat16)
    rest = v - high.astype(jnp.float32)
    mid = rest.astype(jnp.bfloat16)
    low = (rest - mid.astype(jnp.float32)).astype(jnp.bfloat16)
    return high, mid, low


def eliminate(rows, col0, tiles):
    sub = lax.broadcasted_iota(jnp.int32, (ROW, LANE), 0)
    count = len(rows)

    def spread(v, q):
        return jnp.broadcast_to(v[q:q + 1, :], (ROW, LANE))

    for k in range(count):
        lane = (col0 + ROW * k) % LANE
        tc = tiles.index((col0 + ROW * k) // LANE)
        cols = [
            [
                jnp.take_along_axis(
                    rows[i][tc], jnp.full((ROW, LANE), lane + q, jnp.int32), axis=1, mode="promise_in_bounds"
                )
                for i in range(k, count)
            ]
            for q in range(ROW)
        ]
        scale = jnp.zeros((ROW, LANE), jnp.float32)
        for q in range(0, ROW, 2):
            p0, cross, p1 = spread(cols[q][0], q), spread(cols[q][0], q + 1), spread(cols[q + 1][0], q + 1)
            det = p0 * p1 - cross * cross
            inv0 = 1.0 / p0
            inv1 = p0 * (1.0 / det)
            ratio = cross * inv0
            scale = jnp.where(sub == q, lax.rsqrt(p0), scale)
            scale = jnp.where(sub == q + 1, lax.rsqrt(det * inv0), scale)
            m0 = [c * inv0 for c in cols[q]]
            m0[0] = jnp.where(sub > q, m0[0], 0.0)
            m1 = [(c - m * cross) * inv1 for c, m in zip(cols[q + 1], m0)]
            m1[0] = jnp.where(sub > q + 1, m1[0], 0.0)
            for p in range(q + 2, ROW):
                line0 = spread(cols[p][0], q)
                line1 = spread(cols[p][0], q + 1) - ratio * line0
                cols[p] = [(c - a * line0) - b * line1 for c, a, b in zip(cols[p], m0, m1)]
            for t in range(len(tiles)):
                line0 = spread(rows[k][t], q)
                line1 = spread(rows[k][t], q + 1) - ratio * line0
                for i in range(len(m0)):
                    rows[k + i][t] = (rows[k + i][t] - m0[i] * line0) - m1[i] * line1
        for t in range(len(tiles)):
            rows[k][t] = rows[k][t] * scale
    return rows


def factor_kernel(
    mean_hbm, feat_hbm, fac_ref, out_hbm, mean, work, feat, spread_out, packed, mean_sem, feat_sem, out_sems
):
    n = work.shape[0]
    steps = n // PANEL
    top = n // 2
    load = pltpu.make_async_copy(mean_hbm, mean, mean_sem)
    load.start()
    fetch = pltpu.make_async_copy(feat_hbm, feat, feat_sem)
    fetch.start()
    eye_r = lax.broadcasted_iota(jnp.int32, (n, n), 0)
    eye_c = lax.broadcasted_iota(jnp.int32, (n, n), 1)
    work[:, n:] = jnp.where(eye_r == eye_c, 1.0, 0.0)
    left = n // LANE
    blocks = feat.shape[1] // LANE
    stores = []

    def apply(r0, r1, depth):
        count = r1 - r0
        inverse = work[r0:r1, n:n + depth]
        high = inverse.astype(jnp.bfloat16)
        mid = (inverse - high.astype(jnp.float32)).astype(jnp.bfloat16)
        both = jnp.concatenate([high, mid], axis=0)
        chunk = 4
        for j in range(blocks // chunk):
            x = feat[:depth, chunk * LANE * j:chunk * LANE * (j + 1)]
            y = jnp.dot(both, x, preferred_element_type=jnp.float32)
            y = y[:count] + y[count:]
            for b in range(chunk):
                spread_out[pl.ds(r0 * PITCH + j * chunk + b, count, stride=PITCH), :] = y[:, LANE * b:LANE * (b + 1)]
        lines = pl.ds(r0 * blocks, count * blocks)
        wide = spread_out[pl.ds(r0 * PITCH, count * PITCH), :].reshape(count, PITCH, LANE)[:, :blocks]
        packed[lines, :] = wide.reshape(count * blocks, LANE).astype(jnp.bfloat16)
        c = pltpu.make_async_copy(packed.at[lines], out_hbm.at[lines], out_sems.at[len(stores)])
        c.start()
        stores.append(c)

    load.wait()
    parts_of = [mean[h, k] for h in range(2) for k in range(mean.shape[1])]
    e = (mean.shape[2] - 1) // 2
    cross = jnp.concatenate([v[:e] for v in parts_of], axis=0)
    mixed = jnp.concatenate([v[e:2 * e] for v in parts_of], axis=0)
    line = sum(v[2 * e:] for v in parts_of[1:]) + parts_of[0][2 * e:]
    er = lax.broadcasted_iota(jnp.int32, (top, top), 0)
    ec = lax.broadcasted_iota(jnp.int32, (top, top), 1)
    turned = mixed.T
    work[:top, :top] = jnp.where(er >= ec, mixed, turned)
    work[:top, top:n] = cross.T
    work[top:, :top] = cross
    work[top:, top:n] = jnp.where(er == ec, line, jnp.where(ec > er, mixed, turned))
    for p in range(steps):
        r0 = PANEL * p
        first = r0 // LANE
        tiles = list(range(first, left + first + 1))
        rows = [
            [work[r0 + ROW * i:r0 + ROW * (i + 1), LANE * t:LANE * (t + 1)] for t in tiles]
            for i in range(PANEL // ROW)
        ]
        rows = eliminate(rows, r0, tiles)
        whole = jnp.concatenate([jnp.concatenate(r, axis=1) for r in rows], axis=0)
        wide = LANE * (left - first)
        upper = whole[:, :wide]
        rr = r0 + lax.broadcasted_iota(jnp.int32, (PANEL, wide), 0)
        cc = LANE * first + lax.broadcasted_iota(jnp.int32, (PANEL, wide), 1)
        upper = jnp.where(cc >= rr, upper, 0.0)
        lower = upper.T
        fac_ref[LANE * first:, r0:r0 + PANEL] = lower
        if first:
            fac_ref[:LANE * first, r0:r0 + PANEL] = jnp.zeros((LANE * first, PANEL), jnp.float32)
        work[r0:r0 + PANEL, n:n + LANE * (first + 1)] = whole[:, wide:]
        r1 = r0 + PANEL
        if r1 < n:
            high, mid, low = parts(whole)
            right = jnp.concatenate([high, high, high, mid, mid, low], axis=0)
            lh, lm, ll = parts(upper)
            lhs = jnp.concatenate([lh, lm, ll, lh, lm, lh], axis=0).T
            off = LANE * first
            for s0, s1 in ((r1, r1 + PANEL), (r1 + PANEL, n)):
                if s0 < s1:
                    change = jnp.dot(lhs[s0 - off:s1 - off], right, preferred_element_type=jnp.float32)
                    at = LANE * tiles[0]
                    work[s0:s1, at:at + LANE * len(tiles)] -= change
        if p == top // PANEL - 1:
            fetch.wait()
        if p >= top // PANEL and p < steps - 1:
            part = {4: (0, 32), 5: (32, 64), 6: (64, 128)}[p]
            apply(part[0], part[1], top)
    for r0 in range(top, n, n // 4):
        apply(r0, r0 + n // 4, n)
    for c in stores:
        c.wait()


def factor_and_solve(mean, features):
    n, cells = features.shape
    lines = n * cells // LANE
    dma = pltpu.SemaphoreType.DMA
    return pl.pallas_call(
        factor_kernel,
        out_shape=(
            jax.ShapeDtypeStruct((n, n), jnp.float32),
            jax.ShapeDtypeStruct((lines, LANE), jnp.bfloat16),
        ),
        in_specs=[pl.BlockSpec(memory_space=pl.ANY)] * 2,
        out_specs=(pl.BlockSpec(memory_space=pltpu.VMEM), pl.BlockSpec(memory_space=pl.ANY)),
        scratch_shapes=[
            pltpu.VMEM(mean.shape, jnp.float32),
            pltpu.VMEM((n, 2 * n), jnp.float32),
            pltpu.VMEM((n, cells), jnp.bfloat16),
            pltpu.VMEM((n * PITCH, LANE), jnp.float32),
            pltpu.VMEM((lines, LANE), jnp.bfloat16),
            dma, dma, dma((8,)),
        ],
        compiler_params=pltpu.CompilerParams(vmem_limit_bytes=62 << 20),
    )(mean, features)


def spread_mix(mix, snaps, fields, rows):
    ch, count = mix.shape
    group = fields * snaps
    stencils = count // fields
    k = lax.broadcasted_iota(jnp.int32, (count, rows), 0)
    col = lax.broadcasted_iota(jnp.int32, (count, rows), 1)
    pick = (k // stencils == col % group // snaps) & (k % stencils == col // group)
    pick = jnp.where(pick, 1.0, 0.0).astype(jnp.bfloat16)
    r = lax.broadcasted_iota(jnp.int32, (snaps * ch, rows), 0)
    c = lax.broadcasted_iota(jnp.int32, (snaps * ch, rows), 1)
    same = r // ch == c % snaps
    out = []
    for part in parts(mix):
        wide = jnp.dot(part, pick, preferred_element_type=jnp.float32)
        wide = jnp.concatenate([wide] * snaps, axis=0)
        out.append(jnp.where(same, wide, 0.0).astype(jnp.bfloat16))
    return out


def gram_kernel(
    dims, side, steps, count, u_hbm, mix_ref, feat_hbm, out_hbm,
    u_ref, cells, feat, weights, lo, hi,
    stack, pair_in, mine, got_a, got_b, got_y, whole,
    u_sem, feat_sem, out_sem, l_send, l_recv, r_send, r_recv,
    pair_send, pair_recv, a_send, a_recv, b_send, b_recv,
    y_send, y_recv, g_send, g_recv, f_send, f_recv,
):
    fields, snaps, nx, ny = dims
    fs = fields * snaps
    load = pltpu.make_async_copy(u_hbm, u_ref, u_sem)
    load.start()
    here = lax.axis_index("rows")
    t = lax.axis_index("tm")
    size = 2 * side * side
    core = here % 2
    chip = here // 2
    z, x = chip // side, chip % side
    a = (1 - core) * x + core * z
    b = (1 - core) * z + core * x
    a_step = (1 - core) + core * side
    b_step = (1 - core) * side + core
    far = sorted(range(1, side), key=lambda d: -min(d, side - d))
    far_t = sorted(range(1, steps), key=lambda d: -min(d, steps - d))

    def at_a(k):
        return {"rows": 2 * (k * a_step + b * b_step) + core}

    def at_b(k):
        return {"rows": 2 * (a * a_step + k * b_step) + core}

    def at_t(k):
        return {"tm": k}

    partner = {"rows": 2 * chip + 1 - core}

    def copy(src, dst, send, recv, to):
        return pltpu.make_async_remote_copy(
            src_ref=src, dst_ref=dst, send_sem=send, recv_sem=recv,
            device_id=to, device_id_type=MESH,
        )

    left = {"rows": (here + size - 1) % size}
    right = {"rows": (here + 1) % size}
    barrier = pltpu.get_barrier_semaphore()
    for near in (left, right, partner):
        pl.semaphore_signal(barrier, inc=1, device_id=near, device_id_type=MESH)
    for d in range(1, side):
        pl.semaphore_signal(barrier, inc=1, device_id=at_a((a + d) % side), device_id_type=MESH)
        pl.semaphore_signal(barrier, inc=1, device_id=at_b((b + d) % side), device_id_type=MESH)
    for d in range(1, steps):
        pl.semaphore_signal(barrier, inc=1, device_id=at_t((t + d) % steps), device_id_type=MESH)

    rows = 7 * fs + 8
    h, m, l = spread_mix(mix_ref[...], snaps, fields, rows)
    for i, w in enumerate((h, m, l, h, m, h)):
        weights[:, rows * i:rows * (i + 1)] = w

    def at(x, y):
        j = x * ny + y
        return cells[fs * j:fs * (j + 1), :]

    load.wait()
    for j in range(nx * ny):
        cells[fs * j:fs * (j + 1), :] = u_ref[pl.ds(j, fs, stride=nx * ny), :]

    lane = lax.broadcasted_iota(jnp.int32, (fs, LANE), 1)
    zero = jnp.zeros((fs, LANE), jnp.float32)
    pad = jnp.zeros((8, LANE), jnp.float32)

    def plane(x, before, after):
        mid = [at(x, y) for y in range(ny)]
        columns = []
        for y in range(ny):
            u = mid[y]
            xp, xm = after(y), before(y)
            yp = mid[y + 1] if y + 1 < ny else zero
            ym = mid[y - 1] if y else zero
            zp = jnp.where(lane == LANE - 1, 0.0, pltpu.roll(u, LANE - 1, 1))
            zm = jnp.where(lane == 0, 0.0, pltpu.roll(u, 1, 1))
            twice = 2.0 * u
            stencil = jnp.concatenate(
                [
                    u,
                    0.5 * (xp - xm), 0.5 * (yp - ym), 0.5 * (zp - zm),
                    0.25 * (xp - twice + xm), 0.25 * (yp - twice + ym), 0.25 * (zp - twice + zm),
                    pad,
                ],
                axis=0,
            )
            sh, sm, sl = parts(stencil)
            columns.append(jnp.concatenate([sh, sh, sh, sm, sm, sl], axis=0))
        values = jnp.dot(weights[...], jnp.concatenate(columns, axis=1), preferred_element_type=jnp.float32)
        feat[:, ny * LANE * x:ny * LANE * (x + 1)] = values.astype(jnp.bfloat16)

    ahead = 2
    for x in range(1, 1 + ahead):
        plane(x, lambda y: at(x - 1, y), lambda y: at(x + 1, y))

    pl.semaphore_wait(barrier, 2 * (side - 1) + steps + 2)

    block = fs * ny
    go_left = copy(cells.at[pl.ds(0, block)], hi, l_send, l_recv, left)
    go_right = copy(cells.at[pl.ds(block * (nx - 1), block)], lo, r_send, r_recv, right)
    go_left.start()
    go_right.start()
    sends = [go_left, go_right]

    for x in range(1 + ahead, nx - 1):
        plane(x, lambda y: at(x - 1, y), lambda y: at(x + 1, y))

    go_right.wait_recv()
    plane(
        0,
        lambda y: jnp.where(here > 0, lo[fs * y:fs * (y + 1), :], 0.0),
        lambda y: at(1, y),
    )
    go_left.wait_recv()
    plane(
        nx - 1,
        lambda y: at(nx - 2, y),
        lambda y: jnp.where(here < size - 1, hi[fs * y:fs * (y + 1), :], 0.0),
    )

    keep = pltpu.make_async_copy(feat, feat_hbm, feat_sem)
    keep.start()
    f = feat[...]
    gram = lax.dot_general(f, f, (((1,), (1,)), ((), ())), preferred_element_type=jnp.float32)
    edge = gram.shape[0] // 2
    e = (stack.shape[2] - 1) // 2
    er = lax.broadcasted_iota(jnp.int32, (edge, edge), 0)
    ec = lax.broadcasted_iota(jnp.int32, (edge, edge), 1)
    second = gram[edge:, edge:]
    mixed = jnp.where(er >= ec, gram[:edge, :edge], second)
    line = jnp.sum(jnp.where(er == ec, second, 0.0), axis=0, keepdims=True)
    owner = lax.broadcasted_iota(jnp.int32, (1, edge), 1) // e
    for i in range(2 * side):
        stack[i // side, i % side, :e] = gram[edge + e * i:edge + e * (i + 1), :edge]
        stack[i // side, i % side, e:2 * e] = mixed[e * i:e * (i + 1)]
        stack[i // side, i % side, 2 * e:] = jnp.where(owner == i, line, 0.0)

    pair = copy(stack.at[1 - core], pair_in, pair_send, pair_recv, partner)
    pair.start()
    sends.append(pair)
    pair.wait_recv()
    mine[...] = stack[core] + pair_in[...]

    for d in far:
        k = (a + d) % side
        c = copy(mine.at[k], got_a.at[a], a_send.at[d], a_recv.at[a], at_a(k))
        c.start()
        sends.append(c)
    total = mine[a]
    for d in far[::-1]:
        k = (a + d) % side
        copy(mine.at[a], got_a.at[k], a_send.at[d], a_recv.at[k], at_a(k)).wait_recv()
        total = total + got_a[k]
    got_b[b] = total

    for d in far:
        k = (b + d) % side
        c = copy(got_b.at[b], got_b.at[b], b_send.at[d], b_recv.at[b], at_b(k))
        c.start()
        sends.append(c)
    for d in far[::-1]:
        k = (b + d) % side
        copy(got_b.at[b], got_b.at[k], b_send.at[d], b_recv.at[k], at_b(k)).wait_recv()
    total = got_b[0]
    for k in range(1, side):
        total = total + got_b[k]
    got_y[t] = total

    for d in far_t:
        k = t + d

        @pl.when(k < steps)
        def _():
            copy(got_y.at[t], got_y.at[t], y_send.at[d], y_recv.at[t], at_t(k)).start()

    whole[core, a] = jnp.zeros_like(total)
    for k in range(steps):

        @pl.when(k < t)
        def _():
            copy(got_y.at[k], got_y.at[k], y_send.at[0], y_recv.at[k], at_t(k)).wait_recv()

        @pl.when(k <= t)
        def _():
            whole[core, a] += got_y[k]

    whole[core, a] = whole[core, a] / ((t + 1).astype(jnp.float32) * jnp.float32(count))

    def forward(k):
        return copy(whole.at[core, k], whole.at[core, k], f_send.at[k], f_recv.at[k], partner)

    for d in far:
        k = (a + d) % side
        c = copy(whole.at[core, a], whole.at[core, a], g_send.at[d], g_recv.at[a], at_a(k))
        c.start()
        sends.append(c)
    c = forward(a)
    c.start()
    sends.append(c)
    for d in far[::-1]:
        k = (a + d) % side
        copy(whole.at[core, a], whole.at[core, k], g_send.at[d], g_recv.at[k], at_a(k)).wait_recv()
        c = forward(k)
        c.start()
        sends.append(c)
    for k in range(side):
        copy(
            whole.at[core, k], whole.at[1 - core, k], f_send.at[k], f_recv.at[k], partner
        ).wait_recv()

    give = pltpu.make_async_copy(whole, out_hbm, out_sem)
    give.start()
    for c in sends:
        c.wait_send()
    for d in range(1, steps):
        k = t + d

        @pl.when(k < steps)
        def _():
            copy(got_y.at[t], got_y.at[t], y_send.at[d], y_recv.at[t], at_t(k)).wait_send()
    keep.wait()
    give.wait()


def features_and_mean(fields, mix):
    nf, ns, nx, ny, nz = fields.shape
    side = math.isqrt(lax.axis_size("rows") // 2)
    steps = lax.axis_size("tm")
    width = ns * mix.shape[0]
    cells = nx * ny * nz
    rows = 7 * nf * ns + 8
    edge = width // 2
    piece = (side, 2 * (edge // (2 * side)) + 1, edge)
    plane = nf * ns * ny
    dma = pltpu.SemaphoreType.DMA
    f32, bf16 = jnp.float32, jnp.bfloat16
    return pl.pallas_call(
        functools.partial(gram_kernel, (nf, ns, nx, ny), side, steps, cells * lax.axis_size("rows")),
        out_shape=(jax.ShapeDtypeStruct((width, cells), bf16), jax.ShapeDtypeStruct((2,) + piece, f32)),
        in_specs=[pl.BlockSpec(memory_space=pl.ANY), pl.BlockSpec(memory_space=pltpu.VMEM)],
        out_specs=(pl.BlockSpec(memory_space=pl.ANY),) * 2,
        scratch_shapes=[
            pltpu.VMEM((nf * ns * nx * ny, nz), f32),
            pltpu.VMEM((nf * ns * nx * ny, nz), f32),
            pltpu.VMEM((width, cells), bf16),
            pltpu.VMEM((width, 6 * rows), bf16),
            pltpu.VMEM((plane, nz), f32),
            pltpu.VMEM((plane, nz), f32),
            pltpu.VMEM((2,) + piece, f32),
            pltpu.VMEM(piece, f32),
            pltpu.VMEM(piece, f32),
            pltpu.VMEM(piece, f32),
            pltpu.VMEM(piece, f32),
            pltpu.VMEM((steps,) + piece[1:], f32),
            pltpu.VMEM((2,) + piece, f32),
            dma, dma, dma, dma, dma, dma, dma,
            dma, dma,
            dma((side,)), dma((side,)),
            dma((side,)), dma((side,)),
            dma((steps,)), dma((steps,)),
            dma((side,)), dma((side,)),
            dma((side,)), dma((side,)),
        ],
        compiler_params=pltpu.CompilerParams(
            collective_id=0, has_side_effects=True, vmem_limit_bytes=56 << 20
        ),
    )(fields.reshape(-1, nz), mix)


def body(fields, channel_mix):
    features, mean = features_and_mean(fields, channel_mix)
    factor, solved = factor_and_solve(mean, features)
    _, snaps, nx, ny, nz = fields.shape
    coefficients = solved.reshape(snaps, channel_mix.shape[0], nx, ny, nz)
    return (factor[None], coefficients)


def solution(mesh):
    return jax.shard_map(
        body,
        mesh=mesh,
        in_specs=(P(None, "tm", "rows", None, None), P()),
        out_specs=(P("tm", None, None), P("tm", None, "rows", None, None)),
        check_vma=False,
    )
```

```python
import functools
import math

import jax
import jax.numpy as jnp
from jax import lax
from jax.experimental import pallas as pl
from jax.experimental.pallas import tpu as pltpu
from jax.sharding import PartitionSpec as P

MESH = pl.DeviceIdType.MESH
ROW, LANE, PANEL = 8, 128, 32
PITCH = 40


def parts(v):
    high = v.astype(jnp.bfloat16)
    rest = v - high.astype(jnp.float32)
    mid = rest.astype(jnp.bfloat16)
    low = (rest - mid.astype(jnp.float32)).astype(jnp.bfloat16)
    return high, mid, low


def eliminate(rows, col0, tiles):
    sub = lax.broadcasted_iota(jnp.int32, (ROW, LANE), 0)
    count = len(rows)

    def spread(v, q):
        return jnp.broadcast_to(v[q:q + 1, :], (ROW, LANE))

    for k in range(count):
        lane = (col0 + ROW * k) % LANE
        tc = tiles.index((col0 + ROW * k) // LANE)
        cols = [
            [
                jnp.take_along_axis(
                    rows[i][tc], jnp.full((ROW, LANE), lane + q, jnp.int32), axis=1, mode="promise_in_bounds"
                )
                for i in range(k, count)
            ]
            for q in range(ROW)
        ]
        scale = jnp.zeros((ROW, LANE), jnp.float32)
        for q in range(0, ROW, 2):
            p0, cross, p1 = spread(cols[q][0], q), spread(cols[q][0], q + 1), spread(cols[q + 1][0], q + 1)
            det = p0 * p1 - cross * cross
            inv0 = 1.0 / p0
            inv1 = p0 * (1.0 / det)
            ratio = cross * inv0
            scale = jnp.where(sub == q, lax.rsqrt(p0), scale)
            scale = jnp.where(sub == q + 1, lax.rsqrt(det * inv0), scale)
            m0 = [c * inv0 for c in cols[q]]
            m0[0] = jnp.where(sub > q, m0[0], 0.0)
            m1 = [(c - m * cross) * inv1 for c, m in zip(cols[q + 1], m0)]
            m1[0] = jnp.where(sub > q + 1, m1[0], 0.0)
            for p in range(q + 2, ROW):
                line0 = spread(cols[p][0], q)
                line1 = spread(cols[p][0], q + 1) - ratio * line0
                cols[p] = [(c - a * line0) - b * line1 for c, a, b in zip(cols[p], m0, m1)]
            for t in range(len(tiles)):
                line0 = spread(rows[k][t], q)
                line1 = spread(rows[k][t], q + 1) - ratio * line0
                for i in range(len(m0)):
                    rows[k + i][t] = (rows[k + i][t] - m0[i] * line0) - m1[i] * line1
        for t in range(len(tiles)):
            rows[k][t] = rows[k][t] * scale
    return rows


def factor_kernel(
    mean_hbm, feat_hbm, fac_ref, out_hbm, mean, work, feat, spread_out, packed, mean_sem, feat_sem, out_sems
):
    n = work.shape[0]
    steps = n // PANEL
    top = n // 2
    load = pltpu.make_async_copy(mean_hbm, mean, mean_sem)
    load.start()
    fetch = pltpu.make_async_copy(feat_hbm, feat, feat_sem)
    fetch.start()
    eye_r = lax.broadcasted_iota(jnp.int32, (n, n), 0)
    eye_c = lax.broadcasted_iota(jnp.int32, (n, n), 1)
    work[:, n:] = jnp.where(eye_r == eye_c, 1.0, 0.0)
    left = n // LANE
    blocks = feat.shape[1] // LANE
    stores = []

    def apply(r0, r1, depth):
        count = r1 - r0
        inverse = work[r0:r1, n:n + depth]
        high = inverse.astype(jnp.bfloat16)
        mid = (inverse - high.astype(jnp.float32)).astype(jnp.bfloat16)
        both = jnp.concatenate([high, mid], axis=0)
        chunk = 4
        for j in range(blocks // chunk):
            x = feat[:depth, chunk * LANE * j:chunk * LANE * (j + 1)]
            y = jnp.dot(both, x, preferred_element_type=jnp.float32)
            y = y[:count] + y[count:]
            for b in range(chunk):
                spread_out[pl.ds(r0 * PITCH + j * chunk + b, count, stride=PITCH), :] = y[:, LANE * b:LANE * (b + 1)]
        lines = pl.ds(r0 * blocks, count * blocks)
        wide = spread_out[pl.ds(r0 * PITCH, count * PITCH), :].reshape(count, PITCH, LANE)[:, :blocks]
        packed[lines, :] = wide.reshape(count * blocks, LANE).astype(jnp.bfloat16)
        c = pltpu.make_async_copy(packed.at[lines], out_hbm.at[lines], out_sems.at[len(stores)])
        c.start()
        stores.append(c)

    load.wait()
    parts_of = [mean[h, k] for h in range(2) for k in range(mean.shape[1])]
    e = (mean.shape[2] - 1) // 2
    cross = jnp.concatenate([v[:e] for v in parts_of], axis=0)
    mixed = jnp.concatenate([v[e:2 * e] for v in parts_of], axis=0)
    line = sum(v[2 * e:] for v in parts_of[1:]) + parts_of[0][2 * e:]
    er = lax.broadcasted_iota(jnp.int32, (top, top), 0)
    ec = lax.broadcasted_iota(jnp.int32, (top, top), 1)
    turned = mixed.T
    work[:top, :top] = jnp.where(er >= ec, mixed, turned)
    work[:top, top:n] = cross.T
    work[top:, :top] = cross
    work[top:, top:n] = jnp.where(er == ec, line, jnp.where(ec > er, mixed, turned))
    for p in range(steps):
        r0 = PANEL * p
        first = r0 // LANE
        tiles = list(range(first, left + first + 1))
        rows = [
            [work[r0 + ROW * i:r0 + ROW * (i + 1), LANE * t:LANE * (t + 1)] for t in tiles]
            for i in range(PANEL // ROW)
        ]
        rows = eliminate(rows, r0, tiles)
        whole = jnp.concatenate([jnp.concatenate(r, axis=1) for r in rows], axis=0)
        wide = LANE * (left - first)
        upper = whole[:, :wide]
        rr = r0 + lax.broadcasted_iota(jnp.int32, (PANEL, wide), 0)
        cc = LANE * first + lax.broadcasted_iota(jnp.int32, (PANEL, wide), 1)
        upper = jnp.where(cc >= rr, upper, 0.0)
        lower = upper.T
        fac_ref[LANE * first:, r0:r0 + PANEL] = lower
        if first:
            fac_ref[:LANE * first, r0:r0 + PANEL] = jnp.zeros((LANE * first, PANEL), jnp.float32)
        work[r0:r0 + PANEL, n:n + LANE * (first + 1)] = whole[:, wide:]
        r1 = r0 + PANEL
        if r1 < n:
            high, mid, low = parts(whole)
            right = jnp.concatenate([high, high, high, mid, mid, low], axis=0)
            lh, lm, ll = parts(upper)
            lhs = jnp.concatenate([lh, lm, ll, lh, lm, lh], axis=0).T
            off = LANE * first
            for s0, s1 in ((r1, r1 + PANEL), (r1 + PANEL, n)):
                if s0 < s1:
                    change = jnp.dot(lhs[s0 - off:s1 - off], right, preferred_element_type=jnp.float32)
                    at = LANE * tiles[0]
                    work[s0:s1, at:at + LANE * len(tiles)] -= change
        if p == top // PANEL - 1:
            fetch.wait()
        if p >= top // PANEL and p < steps - 1:
            part = {4: (0, 32), 5: (32, 64), 6: (64, 128)}[p]
            apply(part[0], part[1], top)
    for r0 in range(top, n, n // 4):
        apply(r0, r0 + n // 4, n)
    for c in stores:
        c.wait()


def factor_and_solve(mean, features):
    n, cells = features.shape
    lines = n * cells // LANE
    dma = pltpu.SemaphoreType.DMA
    return pl.pallas_call(
        factor_kernel,
        out_shape=(
            jax.ShapeDtypeStruct((n, n), jnp.float32),
            jax.ShapeDtypeStruct((lines, LANE), jnp.bfloat16),
        ),
        in_specs=[pl.BlockSpec(memory_space=pl.ANY)] * 2,
        out_specs=(pl.BlockSpec(memory_space=pltpu.VMEM), pl.BlockSpec(memory_space=pl.ANY)),
        scratch_shapes=[
            pltpu.VMEM(mean.shape, jnp.float32),
            pltpu.VMEM((n, 2 * n), jnp.float32),
            pltpu.VMEM((n, cells), jnp.bfloat16),
            pltpu.VMEM((n * PITCH, LANE), jnp.float32),
            pltpu.VMEM((lines, LANE), jnp.bfloat16),
            dma, dma, dma((8,)),
        ],
        compiler_params=pltpu.CompilerParams(vmem_limit_bytes=62 << 20),
    )(mean, features)


def spread_mix(mix, snaps, fields, rows):
    ch, count = mix.shape
    group = fields * snaps
    stencils = count // fields
    k = lax.broadcasted_iota(jnp.int32, (count, rows), 0)
    col = lax.broadcasted_iota(jnp.int32, (count, rows), 1)
    pick = (k // stencils == col % group // snaps) & (k % stencils == col // group)
    pick = jnp.where(pick, 1.0, 0.0).astype(jnp.bfloat16)
    r = lax.broadcasted_iota(jnp.int32, (snaps * ch, rows), 0)
    c = lax.broadcasted_iota(jnp.int32, (snaps * ch, rows), 1)
    same = r // ch == c % snaps
    out = []
    for part in parts(mix):
        wide = jnp.dot(part, pick, preferred_element_type=jnp.float32)
        wide = jnp.concatenate([wide] * snaps, axis=0)
        out.append(jnp.where(same, wide, 0.0).astype(jnp.bfloat16))
    return out


def gram_kernel(
    dims, side, steps, count, u_hbm, mix_ref, feat_hbm, out_hbm,
    u_ref, cells, feat, weights, lo, hi,
    stack, pair_in, mine, got_a, got_b, got_y, whole,
    u_sem, feat_sem, out_sem, l_send, l_recv, r_send, r_recv,
    pair_send, pair_recv, a_send, a_recv, b_send, b_recv,
    y_send, y_recv, g_send, g_recv, f_send, f_recv,
):
    fields, snaps, nx, ny = dims
    fs = fields * snaps
    load = pltpu.make_async_copy(u_hbm, u_ref, u_sem)
    load.start()
    here = lax.axis_index("rows")
    t = lax.axis_index("tm")
    size = 2 * side * side
    core = here % 2
    chip = here // 2
    z, x = chip // side, chip % side
    a = (1 - core) * x + core * z
    b = (1 - core) * z + core * x
    a_step = (1 - core) + core * side
    b_step = (1 - core) * side + core
    far = sorted(range(1, side), key=lambda d: -min(d, side - d))
    far_t = sorted(range(1, steps), key=lambda d: -min(d, steps - d))

    def at_a(k):
        return {"rows": 2 * (k * a_step + b * b_step) + core}

    def at_b(k):
        return {"rows": 2 * (a * a_step + k * b_step) + core}

    def at_t(k):
        return {"tm": k}

    partner = {"rows": 2 * chip + 1 - core}

    def copy(src, dst, send, recv, to):
        return pltpu.make_async_remote_copy(
            src_ref=src, dst_ref=dst, send_sem=send, recv_sem=recv,
            device_id=to, device_id_type=MESH,
        )

    left = {"rows": (here + size - 1) % size}
    right = {"rows": (here + 1) % size}
    barrier = pltpu.get_barrier_semaphore()
    for near in (left, right, partner):
        pl.semaphore_signal(barrier, inc=1, device_id=near, device_id_type=MESH)
    for d in range(1, side):
        pl.semaphore_signal(barrier, inc=1, device_id=at_a((a + d) % side), device_id_type=MESH)
        pl.semaphore_signal(barrier, inc=1, device_id=at_b((b + d) % side), device_id_type=MESH)
    for d in range(1, steps):
        pl.semaphore_signal(barrier, inc=1, device_id=at_t((t + d) % steps), device_id_type=MESH)

    rows = 7 * fs + 8
    h, m, l = spread_mix(mix_ref[...], snaps, fields, rows)
    for i, w in enumerate((h, m, l, h, m, h)):
        weights[:, rows * i:rows * (i + 1)] = w

    def at(x, y):
        j = x * ny + y
        return cells[fs * j:fs * (j + 1), :]

    load.wait()
    for j in range(nx * ny):
        cells[fs * j:fs * (j + 1), :] = u_ref[pl.ds(j, fs, stride=nx * ny), :]

    lane = lax.broadcasted_iota(jnp.int32, (fs, LANE), 1)
    zero = jnp.zeros((fs, LANE), jnp.float32)
    pad = jnp.zeros((8, LANE), jnp.float32)

    def plane(x, before, after):
        mid = [at(x, y) for y in range(ny)]
        columns = []
        for y in range(ny):
            u = mid[y]
            xp, xm = after(y), before(y)
            yp = mid[y + 1] if y + 1 < ny else zero
            ym = mid[y - 1] if y else zero
            zp = jnp.where(lane == LANE - 1, 0.0, pltpu.roll(u, LANE - 1, 1))
            zm = jnp.where(lane == 0, 0.0, pltpu.roll(u, 1, 1))
            twice = 2.0 * u
            stencil = jnp.concatenate(
                [
                    u,
                    0.5 * (xp - xm), 0.5 * (yp - ym), 0.5 * (zp - zm),
                    0.25 * (xp - twice + xm), 0.25 * (yp - twice + ym), 0.25 * (zp - twice + zm),
                    pad,
                ],
                axis=0,
            )
            sh, sm, sl = parts(stencil)
            columns.append(jnp.concatenate([sh, sh, sh, sm, sm, sl], axis=0))
        values = jnp.dot(weights[...], jnp.concatenate(columns, axis=1), preferred_element_type=jnp.float32)
        feat[:, ny * LANE * x:ny * LANE * (x + 1)] = values.astype(jnp.bfloat16)

    ahead = 2
    for x in range(1, 1 + ahead):
        plane(x, lambda y: at(x - 1, y), lambda y: at(x + 1, y))

    pl.semaphore_wait(barrier, 2 * (side - 1) + steps + 2)

    block = fs * ny
    go_left = copy(cells.at[pl.ds(0, block)], hi, l_send, l_recv, left)
    go_right = copy(cells.at[pl.ds(block * (nx - 1), block)], lo, r_send, r_recv, right)
    go_left.start()
    go_right.start()
    sends = [go_left, go_right]

    for x in range(1 + ahead, nx - 1):
        plane(x, lambda y: at(x - 1, y), lambda y: at(x + 1, y))

    go_right.wait_recv()
    plane(
        0,
        lambda y: jnp.where(here > 0, lo[fs * y:fs * (y + 1), :], 0.0),
        lambda y: at(1, y),
    )
    go_left.wait_recv()
    plane(
        nx - 1,
        lambda y: at(nx - 2, y),
        lambda y: jnp.where(here < size - 1, hi[fs * y:fs * (y + 1), :], 0.0),
    )

    keep = pltpu.make_async_copy(feat, feat_hbm, feat_sem)
    keep.start()
    f = feat[...]
    gram = lax.dot_general(f, f, (((1,), (1,)), ((), ())), preferred_element_type=jnp.float32)
    edge = gram.shape[0] // 2
    e = (stack.shape[2] - 1) // 2
    er = lax.broadcasted_iota(jnp.int32, (edge, edge), 0)
    ec = lax.broadcasted_iota(jnp.int32, (edge, edge), 1)
    second = gram[edge:, edge:]
    mixed = jnp.where(er >= ec, gram[:edge, :edge], second)
    line = jnp.sum(jnp.where(er == ec, second, 0.0), axis=0, keepdims=True)
    owner = lax.broadcasted_iota(jnp.int32, (1, edge), 1) // e
    for i in range(2 * side):
        stack[i // side, i % side, :e] = gram[edge + e * i:edge + e * (i + 1), :edge]
        stack[i // side, i % side, e:2 * e] = mixed[e * i:e * (i + 1)]
        stack[i // side, i % side, 2 * e:] = jnp.where(owner == i, line, 0.0)

    pair = copy(stack.at[1 - core], pair_in, pair_send, pair_recv, partner)
    pair.start()
    sends.append(pair)
    pair.wait_recv()
    mine[...] = stack[core] + pair_in[...]

    for d in far:
        k = (a + d) % side
        c = copy(mine.at[k], got_a.at[a], a_send.at[d], a_recv.at[a], at_a(k))
        c.start()
        sends.append(c)
    total = mine[a]
    for d in far[::-1]:
        k = (a + d) % side
        copy(mine.at[a], got_a.at[k], a_send.at[d], a_recv.at[k], at_a(k)).wait_recv()
        total = total + got_a[k]
    got_b[b] = total

    for d in far:
        k = (b + d) % side
        c = copy(got_b.at[b], got_b.at[b], b_send.at[d], b_recv.at[b], at_b(k))
        c.start()
        sends.append(c)
    for d in far[::-1]:
        k = (b + d) % side
        copy(got_b.at[b], got_b.at[k], b_send.at[d], b_recv.at[k], at_b(k)).wait_recv()
    total = got_b[0]
    for k in range(1, side):
        total = total + got_b[k]
    got_y[t] = total

    for d in far_t:
        k = (t + d) % steps
        c = copy(got_y.at[t], got_y.at[t], y_send.at[d], y_recv.at[t], at_t(k))
        c.start()
        sends.append(c)
    for d in far_t[::-1]:
        k = (t + d) % steps
        copy(got_y.at[t], got_y.at[k], y_send.at[d], y_recv.at[k], at_t(k)).wait_recv()
    total = got_y[0]
    for k in range(1, steps):
        total = total + jnp.where(k <= t, got_y[k], 0.0)
    whole[core, a] = total / ((t + 1).astype(jnp.float32) * jnp.float32(count))

    def forward(k):
        return copy(whole.at[core, k], whole.at[core, k], f_send.at[k], f_recv.at[k], partner)

    for d in far:
        k = (a + d) % side
        c = copy(whole.at[core, a], whole.at[core, a], g_send.at[d], g_recv.at[a], at_a(k))
        c.start()
        sends.append(c)
    c = forward(a)
    c.start()
    sends.append(c)
    for d in far[::-1]:
        k = (a + d) % side
        copy(whole.at[core, a], whole.at[core, k], g_send.at[d], g_recv.at[k], at_a(k)).wait_recv()
        c = forward(k)
        c.start()
        sends.append(c)
    for k in range(side):
        copy(
            whole.at[core, k], whole.at[1 - core, k], f_send.at[k], f_recv.at[k], partner
        ).wait_recv()

    give = pltpu.make_async_copy(whole, out_hbm, out_sem)
    give.start()
    for c in sends:
        c.wait_send()
    keep.wait()
    give.wait()


def features_and_mean(fields, mix):
    nf, ns, nx, ny, nz = fields.shape
    side = math.isqrt(lax.axis_size("rows") // 2)
    steps = lax.axis_size("tm")
    width = ns * mix.shape[0]
    cells = nx * ny * nz
    rows = 7 * nf * ns + 8
    edge = width // 2
    piece = (side, 2 * (edge // (2 * side)) + 1, edge)
    plane = nf * ns * ny
    dma = pltpu.SemaphoreType.DMA
    f32, bf16 = jnp.float32, jnp.bfloat16
    return pl.pallas_call(
        functools.partial(gram_kernel, (nf, ns, nx, ny), side, steps, cells * lax.axis_size("rows")),
        out_shape=(jax.ShapeDtypeStruct((width, cells), bf16), jax.ShapeDtypeStruct((2,) + piece, f32)),
        in_specs=[pl.BlockSpec(memory_space=pl.ANY), pl.BlockSpec(memory_space=pltpu.VMEM)],
        out_specs=(pl.BlockSpec(memory_space=pl.ANY),) * 2,
        scratch_shapes=[
            pltpu.VMEM((nf * ns * nx * ny, nz), f32),
            pltpu.VMEM((nf * ns * nx * ny, nz), f32),
            pltpu.VMEM((width, cells), bf16),
            pltpu.VMEM((width, 6 * rows), bf16),
            pltpu.VMEM((plane, nz), f32),
            pltpu.VMEM((plane, nz), f32),
            pltpu.VMEM((2,) + piece, f32),
            pltpu.VMEM(piece, f32),
            pltpu.VMEM(piece, f32),
            pltpu.VMEM(piece, f32),
            pltpu.VMEM(piece, f32),
            pltpu.VMEM((steps,) + piece[1:], f32),
            pltpu.VMEM((2,) + piece, f32),
            dma, dma, dma, dma, dma, dma, dma,
            dma, dma,
            dma((side,)), dma((side,)),
            dma((side,)), dma((side,)),
            dma((steps,)), dma((steps,)),
            dma((side,)), dma((side,)),
            dma((side,)), dma((side,)),
        ],
        compiler_params=pltpu.CompilerParams(
            collective_id=0, has_side_effects=True, vmem_limit_bytes=56 << 20
        ),
    )(fields.reshape(-1, nz), mix)


def body(fields, channel_mix):
    features, mean = features_and_mean(fields, channel_mix)
    factor, solved = factor_and_solve(mean, features)
    _, snaps, nx, ny, nz = fields.shape
    coefficients = solved.reshape(snaps, channel_mix.shape[0], nx, ny, nz)
    return (factor[None], coefficients)


def solution(mesh):
    return jax.shard_map(
        body,
        mesh=mesh,
        in_specs=(P(None, "tm", "rows", None, None), P()),
        out_specs=(P("tm", None, None), P("tm", None, "rows", None, None)),
        check_vma=False,
    )
```
